256 devices in a mesh: ctx: 256 (over x, y, z, core).
Axes of the slice: x: 4, y: 4, z: 8, core: 2. Of those that a mesh axis runs over, the one named last changes fastest.
Arguments:
- queries: bfloat16 [32768, 512], P('ctx'), may hold values from -6 to 6
- keys: bfloat16 [32768, 512], P('ctx'), may hold values from -6 to 6
- values: bfloat16 [32768, 512], P('ctx'), may hold values from -6 to 6
- out_weight: bfloat16 [4096, 512], P('ctx'), may hold values from -0.25 to 0.25
- cotangent: bfloat16 [32768, 4096], P('ctx'), may hold values from -24 to 24
Outputs:
- mixed: bfloat16 [32768, 4096], P('ctx')
- query_gradient: bfloat16 [32768, 512], P('ctx')
- key_gradient: bfloat16 [32768, 512], P('ctx')
- value_gradient: bfloat16 [32768, 512], P('ctx')
- weight_grad: float32 [4096, 512], P('ctx')
The draws below stay inside these ranges and needn't reach their ends.
All inputs are finite; a program needn't handle non-finite values.
Results may differ from the reference program's by a relative error of at most 0.014.
Values may be sent and summed in bfloat16 or wider, within the bound.
No kernel may reach another device: no remote copies, remote signals or barrier semaphores. Data moves between devices by JAX's collectives and lax.ppermute only.
A program may use at most 320 MiB of HBM per device.

```python
import jax
import jax.numpy as jnp
from jax import lax

D = 4096
HEADS = 4
HEAD = 128
HF = 512
TOK_DEV = 128
TOKENS = 32768
N_CTX = 256


def spiked(result, rng, source, target, blocks, factor):
    def block_of(position):
        return (jnp.arange(result.shape[position]) // (result.shape[position] // blocks)).reshape((-1,) + (1,) * (result.ndim - 1 - position))

    one_side = jax.random.permutation(rng, blocks)[block_of(target)]
    other_side = (block_of(target) + blocks // 2) % blocks
    return jnp.where((block_of(source) == one_side) | (block_of(source) == other_side), factor * result, result)


def level_of(stream_key, dims, split, smallest, high):
    factor_of, own = 1.0, jax.random.fold_in(stream_key, 6)
    for axis_at, blocks in split:
        heights = jnp.exp(jax.random.uniform(jax.random.fold_in(own, axis_at), (blocks,), jnp.float32, smallest / len(split), high / len(split)))
        factor_of = factor_of * jnp.repeat(heights, dims[axis_at] // blocks).reshape([-1 if axis == axis_at else 1 for axis in range(len(dims))])
    return factor_of


def bell_draw(own_key, extent, scale, most, split=(), held_as=jnp.bfloat16):
    result = scale * jax.random.normal(own_key, extent, jnp.float32)
    if split:
        result = result * level_of(own_key, extent, split, -0.22, 0.18)
    return jnp.clip(result, -most, most).astype(held_as)


def bell_draw_with(rng, dims, scale, reach, split, heavy, held_as=jnp.bfloat16):
    array = scale * jax.random.normal(rng, dims, jnp.float32)
    if split:
        array = array * level_of(rng, dims, split, -0.22, 0.18)
    return jnp.clip(spiked(array, jax.random.fold_in(rng, 3), *heavy), -reach, reach).astype(held_as)


def setup_inputs(seed: int = 0) -> dict:
    key_list = jax.random.split(jax.random.key(seed), 6)
    return {
        "queries": bell_draw(key_list[0], (TOKENS, HF), 1.0, 6.0, ((0, 256),)),
        "keys": bell_draw(key_list[1], (TOKENS, HF), 1.0, 6.0, ((0, 256),)),
        "values": bell_draw(key_list[2], (TOKENS, HF), 1.0, 6.0, ((0, 256),)),
        "out_weight": bell_draw(key_list[3], (D, HF), HF ** -0.5, 0.25, ((0, 256),)),
        "cotangent": bell_draw_with(key_list[4], (TOKENS, D), 1.0, 24.0, ((0, 256),), (0, 1, 256, 6.0)),
    }


def block_terms(items):
    head_queries, head_keys, head_values, head_gradient, prefix_key_state, state_gradient, position_scale = items
    query_wide = head_queries.astype(jnp.float32)
    key_wide = head_keys.astype(jnp.float32)
    value_wide = head_values.astype(jnp.float32)
    gradient_wide = head_gradient.astype(jnp.float32)
    prefix_key_state_wide = prefix_key_state.astype(jnp.float32)
    state_gradient_wide = state_gradient.astype(jnp.float32)
    row_index = jnp.arange(TOK_DEV, dtype=jnp.int32)
    causal = (row_index[:, None] >= row_index[None, :])[None]
    scores = jnp.einsum('shd,thd->hst', query_wide, key_wide)
    masked_scores = jnp.where(causal, scores, 0.0).astype(jnp.bfloat16).astype(jnp.float32)
    local_part = jnp.einsum('kun,nkr->ukr', masked_scores, value_wide)
    carried_over = jnp.einsum('mqw,qwi->mqi', query_wide, prefix_key_state_wide)
    attended = ((local_part + carried_over) * position_scale[:, None, None]).astype(jnp.bfloat16)
    grad_scores = jnp.einsum('shd,thd->hst', gradient_wide, value_wide)
    masked_gradient = jnp.where(causal, grad_scores, 0.0).astype(jnp.bfloat16).astype(jnp.float32)
    query_gradient = jnp.einsum('kun,nkr->ukr', masked_gradient, key_wide) + jnp.einsum('riq,ipq->rip', gradient_wide, prefix_key_state_wide)
    key_gradient = jnp.einsum('olf,loy->foy', masked_gradient, query_wide) + jnp.einsum('rwd,wed->rwe', value_wide, state_gradient_wide)
    value_gradient = jnp.einsum('olf,loy->foy', masked_scores, gradient_wide) + jnp.einsum('pyd,yda->pya', key_wide, state_gradient_wide)
    return (attended, query_gradient.astype(jnp.bfloat16), key_gradient.astype(jnp.bfloat16), value_gradient.astype(jnp.bfloat16))

def reference(queries, keys, values, out_weight, cotangent):
    positions = jnp.arange(TOKENS, dtype=jnp.int32)
    position_scale = lax.rsqrt(HEAD * (positions + 1).astype(jnp.float32))
    grad_attended = jnp.dot(cotangent, out_weight, preferred_element_type=jnp.float32)
    scaled_grad = (grad_attended * position_scale[:, None]).astype(jnp.bfloat16)
    shape_four = (N_CTX, TOK_DEV, HEADS, HEAD)
    query_blocks = queries.reshape(shape_four)
    key_blocks = keys.reshape(shape_four)
    value_blocks = values.reshape(shape_four)
    grad_blocks = scaled_grad.reshape(shape_four)
    local_keys = jnp.einsum('bthk,bthv->bhkv', key_blocks.astype(jnp.float32), value_blocks.astype(jnp.float32))
    local_grads = jnp.einsum('bthk,bthv->bhkv', query_blocks.astype(jnp.float32), grad_blocks.astype(jnp.float32))
    running_keys = jnp.cumsum(local_keys, axis=0)
    prefix_key_state = (running_keys - local_keys).astype(jnp.bfloat16)
    running_grads = jnp.cumsum(local_grads, axis=0)
    state_gradient = (running_grads[-1][None] - running_grads).astype(jnp.bfloat16)
    scale_blocks = position_scale.reshape(N_CTX, TOK_DEV)
    attended, query_gradient, key_gradient, value_gradient = lax.map(block_terms, (query_blocks, key_blocks, value_blocks, grad_blocks, prefix_key_state, state_gradient, scale_blocks))
    attended = attended.reshape(TOKENS, HF)
    mixed = lax.dot_general(attended, out_weight, (((1,), (1,)), ((), ())), preferred_element_type=jnp.float32).astype(jnp.bfloat16)
    weight_grad = lax.dot_general(cotangent, attended, (((0,), (0,)), ((), ())), preferred_element_type=jnp.float32)
    return (mixed, query_gradient.reshape(TOKENS, HF), key_gradient.reshape(TOKENS, HF), value_gradient.reshape(TOKENS, HF), weight_grad)
```

```python
import jax
import jax.numpy as jnp
from jax import lax
from jax.sharding import Mesh, PartitionSpec as P

HEADS = 4
HEAD = 128
XY = ("x", "y")
ZC = ("z", "c")
BF16 = jnp.bfloat16
F32 = jnp.float32


def exchange(value, axes):
    return lax.all_to_all(value, axes, 0, 0, tiled=True)


def earlier_sums(parts):
    running = jnp.zeros(parts.shape[1:], F32)
    before = []
    for i in range(parts.shape[0]):
        before.append(running)
        running = running + parts[i].astype(F32)
    return jnp.stack(before), running


def later_sums(parts):
    running = jnp.zeros(parts.shape[1:], F32)
    after = []
    for i in reversed(range(parts.shape[0])):
        after.append(running)
        running = running + parts[i].astype(F32)
    return jnp.stack(after[::-1]), running


def masked_sum(parts, keep):
    return jnp.sum(jnp.where(keep[:, None, None], parts.astype(F32), 0.0), axis=0)


def body(queries, keys, values, out_weight, cotangent):
    groups = lax.axis_size(XY)
    members = lax.axis_size(ZC)
    group = lax.axis_index(XY)
    member = lax.axis_index(ZC)
    core = lax.axis_index("c")
    tokens, features = queries.shape
    rows = out_weight.shape[0]
    model = cotangent.shape[1]
    half = features // 2
    state_rows = HEADS * HEAD // members
    offset = (group * members + member) * tokens
    positions = offset + jnp.arange(tokens, dtype=jnp.int32)
    position_scale = lax.rsqrt(HEAD * (positions + 1).astype(F32))
    swap = [(0, 1), (1, 0)]

    column = exchange(jnp.broadcast_to(out_weight[None], (groups,) + out_weight.shape), XY)
    full_weight = lax.all_gather(column, ZC, axis=0)
    other_cotangent = lax.ppermute(cotangent, "c", swap)

    head_shape = (tokens, HEADS, HEAD)
    head_queries = queries.reshape(head_shape)
    head_keys = keys.reshape(head_shape)
    head_values = values.reshape(head_shape)

    local_keys = jnp.einsum("ixj,ixg->xjg", head_keys, head_values, preferred_element_type=F32)
    first = exchange(local_keys.astype(BF16).reshape(members, state_rows, HEAD), ZC)
    inside, total = earlier_sums(first)
    second = exchange(jnp.broadcast_to(total.astype(BF16)[None], (groups, state_rows, HEAD)), XY)
    before = masked_sum(second, jnp.arange(groups) < group)
    key_state = exchange((inside + before[None]).astype(BF16), ZC).reshape(HEADS, HEAD, HEAD)

    row_index = jnp.arange(tokens, dtype=jnp.int32)
    causal = (row_index[:, None] >= row_index[None, :])[None]
    scores = jnp.einsum("shd,thd->hst", head_queries, head_keys, preferred_element_type=F32)
    scores = jnp.where(causal, scores, 0.0).astype(BF16)
    local_part = jnp.einsum("kun,nkr->ukr", scores, head_values, preferred_element_type=F32)
    carried = jnp.einsum("mqw,qwi->mqi", head_queries, key_state, preferred_element_type=F32)
    attended = ((local_part + carried) * position_scale[:, None, None]).astype(BF16)
    attended = attended.reshape(tokens, features)

    full_weight = full_weight.transpose(1, 0, 2, 3).reshape(model, features)
    grad_attended = jnp.dot(cotangent, full_weight, preferred_element_type=F32)
    scaled_grad = (grad_attended * position_scale[:, None]).astype(BF16)
    head_gradient = scaled_grad.reshape(head_shape)
    local_grads = jnp.einsum("ixj,ixg->xjg", head_queries, head_gradient, preferred_element_type=F32)
    first = exchange(local_grads.astype(BF16).reshape(members, state_rows, HEAD), ZC)
    inside, total = later_sums(first)

    mine = lax.dynamic_slice_in_dim(attended, core * half, half, 1)
    theirs = lax.dynamic_slice_in_dim(attended, (1 - core) * half, half, 1)
    other = lax.ppermute(theirs, "c", swap)
    contract = (((0,), (0,)), ((), ()))
    weight_term = lax.dot_general(cotangent, mine, contract, preferred_element_type=F32)
    weight_term = weight_term + lax.dot_general(other_cotangent, other, contract, preferred_element_type=F32)
    weight_term = weight_term.astype(BF16).reshape(groups, model // groups, half)
    pack = state_rows * HEAD // half
    total = jnp.broadcast_to(total.astype(BF16).reshape(1, pack, half), (groups, pack, half))
    second = exchange(jnp.concatenate([weight_term, total], axis=1), XY)
    share = model // groups
    after = masked_sum(second[:, share:].reshape(groups, state_rows, HEAD), jnp.arange(groups) > group)
    weight_part = jnp.sum(second[:, :share].astype(F32), axis=0).astype(BF16).reshape(members, rows, half)
    states = (inside + after[None]).astype(BF16).reshape(members, pack, half)
    third = exchange(jnp.concatenate([weight_part, states], axis=1), ZC)
    grad_state = third[:, rows:].reshape(HEADS, HEAD, HEAD)
    weight_grad = jnp.sum(third[:, :rows].astype(F32).reshape(members // 2, 2, rows, half), axis=0)
    weight_grad = weight_grad.transpose(1, 0, 2).reshape(rows, features)

    mixed = lax.dot_general(
        attended, full_weight, (((1,), (1,)), ((), ())), preferred_element_type=F32
    ).astype(BF16)
    grad_scores = jnp.einsum("shd,thd->hst", head_gradient, head_values, preferred_element_type=F32)
    grad_scores = jnp.where(causal, grad_scores, 0.0).astype(BF16)
    query_gradient = jnp.einsum("kun,nkr->ukr", grad_scores, head_keys, preferred_element_type=F32)
    query_gradient += jnp.einsum("riq,ipq->rip", head_gradient, key_state, preferred_element_type=F32)
    key_gradient = jnp.einsum("olf,loy->foy", grad_scores, head_queries, preferred_element_type=F32)
    key_gradient += jnp.einsum("rwd,wed->rwe", head_values, grad_state, preferred_element_type=F32)
    value_gradient = jnp.einsum("olf,loy->foy", scores, head_gradient, preferred_element_type=F32)
    value_gradient += jnp.einsum("pyd,yda->pya", head_keys, grad_state, preferred_element_type=F32)
    flat = (tokens, features)
    query_gradient = query_gradient.reshape(flat).astype(BF16)
    key_gradient = key_gradient.reshape(flat).astype(BF16)
    value_gradient = value_gradient.reshape(flat).astype(BF16)
    return (mixed, query_gradient, key_gradient, value_gradient, weight_grad)


def solution(mesh):
    grid = Mesh(mesh.devices.reshape(4, 4, 8, 2), ("x", "y", "z", "c"))
    spec = P(("x", "y", "z", "c"), None)
    return jax.shard_map(
        body, mesh=grid, in_specs=(spec,) * 5, out_specs=(spec,) * 5, check_vma=False
    )
```

```python
import functools

import jax
import jax.numpy as jnp
from jax import lax
from jax.experimental import pallas as pl
from jax.experimental.pallas import tpu as pltpu
from jax.sharding import Mesh, PartitionSpec as P

HEADS = 4
HEAD = 128
TOKENS = 128
FEATURES = HEADS * HEAD
MODEL = 4096
GROUPS = 16
MEMBERS = 16
ROWS = MODEL // (GROUPS * MEMBERS)
SHARE = MODEL // GROUPS
STATE_ROWS = FEATURES // MEMBERS
CHUNKS = 4
XY = ("x", "y")
ZC = ("z", "c")
BF16 = jnp.bfloat16
F32 = jnp.float32
NN = (((1,), (0,)), ((), ()))
NT = (((1,), (1,)), ((), ()))
TN = (((0,), (0,)), ((), ()))
VMEM = pl.BlockSpec(memory_space=pltpu.VMEM)
SMEM = pl.BlockSpec(memory_space=pltpu.SMEM)
HBM = pl.BlockSpec(memory_space=pltpu.HBM)


def mul(a, b, dims):
    return lax.dot_general(a, b, dims, preferred_element_type=F32)


def shape(dims, dtype):
    return jax.ShapeDtypeStruct(dims, dtype)


def call(kernel, ins, outs, args, flops, limit=32, **kw):
    out_bytes = sum(o.size * o.dtype.itemsize for o in outs)
    in_bytes = sum(a.size * a.dtype.itemsize for a in args)
    one = len(outs) == 1
    return pl.pallas_call(
        kernel,
        in_specs=ins,
        out_specs=VMEM if one else [VMEM] * len(outs),
        out_shape=outs[0] if one else outs,
        compiler_params=pltpu.CompilerParams(vmem_limit_bytes=limit << 20),
        cost_estimate=pl.CostEstimate(
            flops=flops, bytes_accessed=in_bytes + out_bytes, transcendentals=0
        ),
        **kw,
    )(*args)


def head(ref, h):
    return ref[:, h * HEAD : (h + 1) * HEAD]


def state(ref, h):
    return ref[h * HEAD : (h + 1) * HEAD, :]


def causal(x):
    row = lax.broadcasted_iota(jnp.int32, x.shape, 0)
    col = lax.broadcasted_iota(jnp.int32, x.shape, 1)
    return jnp.where(row >= col, x, 0.0).astype(BF16)


def keys_kernel(k, v, out):
    for h in range(HEADS):
        out[h * HEAD : (h + 1) * HEAD, :] = mul(head(k, h), head(v, h), TN).astype(BF16)


def attend_kernel(place, q, k, v, key_state, scale, out, own, out_c, out_y, out_yc, by_head):
    for h in range(HEADS):
        qh = head(q, h)
        scores = causal(mul(qh, head(k, h), NT))
        total = mul(scores, head(v, h), NN) + mul(qh, state(key_state, h), NN)
        result = (total * scale[...]).astype(BF16)
        out[:, h * HEAD : (h + 1) * HEAD] = result
        by_head[h] = result
    me = place[0]
    own[...] = by_head[me]
    out_c[...] = by_head[me ^ 2]
    out_y[...] = by_head[me ^ 1]
    out_yc[...] = by_head[me ^ 3]


def weight_copies(w, held, sems):
    part = GROUPS // CHUNKS
    copies = []
    for i in range(CHUNKS):
        at = pl.ds(i * part, part)
        copies.append(pltpu.make_async_copy(w.at[:, at], held.at[:, at], sems.at[i]))
    return copies


def share_of(held, j):
    return held[:, j].reshape(SHARE, FEATURES)


def gradient_kernel(cot, w, q, scale, grad, sums, held, sems, cots, cot_sem):
    cot_copy = pltpu.make_async_copy(cot, cots, cot_sem)
    cot_copy.start()
    copies = weight_copies(w, held, sems)
    for copy in copies:
        copy.start()
    cot_copy.wait()
    total = None
    part = GROUPS // CHUNKS
    for i in range(CHUNKS):
        copies[i].wait()
        rows = [share_of(held, j) for j in range(i * part, (i + 1) * part)]
        at = slice(i * part * SHARE, (i + 1) * part * SHARE)
        term = mul(cots[:, at], jnp.concatenate(rows, axis=0), NN)
        total = term if total is None else total + term
    g = (total * scale[...]).astype(BF16)
    grad[...] = g
    for h in range(HEADS):
        gh = g[:, h * HEAD : (h + 1) * HEAD]
        sums[h * HEAD : (h + 1) * HEAD, :] = mul(head(q, h), gh, TN).astype(BF16)


def mixed_kernel(att, w, out, held, sems):
    copies = weight_copies(w, held, sems)
    for copy in copies:
        copy.start()
    for j in range(GROUPS):
        if j % (GROUPS // CHUNKS) == 0:
            copies[j // (GROUPS // CHUNKS)].wait()
        out[:, j * SHARE : (j + 1) * SHARE] = mul(att[...], share_of(held, j), NT).astype(BF16)


def weight_kernel(c0, c1, c2, c3, c4, c5, a0, a1, a2, a3, out):
    turned = jnp.concatenate([a[...].T for a in (a0, a1, a2, a3)], axis=1)
    for j in range(out.shape[0]):
        at = slice(j * SHARE, (j + 1) * SHARE)
        cots = jnp.concatenate([c[:, at] for c in (c0, c1, c2, c3, c4, c5)], axis=0)
        term = mul(turned, cots, NN).astype(BF16)
        for half in range(2):
            out[j, half * HEAD : (half + 1) * HEAD, :] = term[:, half * HEAD : (half + 1) * HEAD]
        out[j, SHARE:, :] = jnp.zeros((STATE_ROWS, HEAD), BF16)


def local_kernel(q, k, v, g, key_state, qg, kg, vg):
    for h in range(HEADS):
        at = slice(h * HEAD, (h + 1) * HEAD)
        qh, kh, vh, gh = head(q, h), head(k, h), head(v, h), head(g, h)
        scores = causal(mul(qh, kh, NT))
        grads = causal(mul(gh, vh, NT))
        qg[:, at] = (mul(grads, kh, NN) + mul(gh, state(key_state, h), NT)).astype(BF16)
        kg[:, at] = mul(grads, qh, TN)
        vg[:, at] = mul(scores, gh, TN)


def reduce_kernel(group, got, inside, out):
    me = group[0]
    after = jnp.zeros((STATE_ROWS, HEAD), F32)
    for j in range(GROUPS):
        piece = got[j, SHARE:, :].astype(F32)
        after = after + jnp.where(j > me, piece, 0.0)
    for m in range(MEMBERS):
        out[m, 2 * ROWS :, :] = (inside[m] + after).astype(BF16)
    for odd in range(2):
        for half in range(2):
            total = None
            for j in range(odd, GROUPS, 2):
                piece = got[j, half * HEAD : (half + 1) * HEAD, :].astype(F32)
                total = piece if total is None else total + piece
            turned = total.T.astype(BF16)
            for m in range(HEAD // ROWS):
                out[half * (HEAD // ROWS) + m, odd * ROWS : (odd + 1) * ROWS, :] = turned[
                    m * ROWS : (m + 1) * ROWS
                ]


def final_kernel(got, k, v, kg_local, vg_local, kg, vg, wg):
    per = HEAD // STATE_ROWS
    for h in range(HEADS):
        at = slice(h * HEAD, (h + 1) * HEAD)
        grad_state = jnp.concatenate(
            [got[h * per + i, 2 * ROWS :, :] for i in range(per)], axis=0
        )
        kg[:, at] = (kg_local[:, at] + mul(head(v, h), grad_state, NT)).astype(BF16)
        vg[:, at] = (vg_local[:, at] + mul(head(k, h), grad_state, NN)).astype(BF16)
    for core in range(2):
        for odd in range(2):
            total = None
            for m in range(core, MEMBERS, 2):
                piece = got[m, odd * ROWS : (odd + 1) * ROWS, :].astype(F32)
                total = piece if total is None else total + piece
            at = (core * 2 + odd) * HEAD
            wg[:, at : at + HEAD] = total


def exchange(value, axes):
    return lax.all_to_all(value, axes, 0, 0, tiled=True)


def sums_before(parts):
    running, before = jnp.zeros(parts[0].shape, F32), []
    for part in parts:
        before.append(running)
        running = running + part.astype(F32)
    return before, running


def body(queries, keys, values, out_weight, cotangent):
    group = lax.axis_index(XY)
    member = lax.axis_index(ZC)
    core = lax.axis_index("c")
    odd = lax.rem(lax.axis_index("y"), 2)
    positions = (group * MEMBERS + member) * TOKENS + jnp.arange(TOKENS, dtype=jnp.int32)
    scale = lax.rsqrt(HEAD * (positions + 1).astype(F32))[:, None]
    swap = [(0, 1), (1, 0)]
    swap_y = [(0, 1), (1, 0), (2, 3), (3, 2)]
    rows_shape = (MEMBERS, STATE_ROWS, HEAD)
    small = 2 * TOKENS * HEAD * FEATURES
    large = 2 * TOKENS * MODEL * FEATURES

    local_keys = call(
        keys_kernel, [VMEM] * 2, [shape((FEATURES, HEAD), BF16)], (keys, values), small
    )
    column = exchange(jnp.broadcast_to(out_weight[None], (GROUPS, ROWS, FEATURES)), XY)
    column, local_keys = lax.optimization_barrier((column, local_keys))
    weight = lax.all_gather(column, ZC, axis=0)
    cot_c = lax.ppermute(cotangent, "c", swap)
    cot_y1 = lax.ppermute(cotangent[: TOKENS // 2], "y", swap_y)

    first = exchange(local_keys.reshape(rows_shape), ZC)
    before, total = sums_before([first[i] for i in range(MEMBERS)])
    second = exchange(jnp.broadcast_to(total.astype(BF16)[None], rows_shape), XY)
    earlier = (jnp.arange(GROUPS) < group)[:, None, None]
    carried = jnp.sum(jnp.where(earlier, second.astype(F32), 0.0), axis=0)
    states = (jnp.stack(before) + carried[None]).astype(BF16)
    states, cot_c, cot_y1, late = lax.optimization_barrier(
        (states, cot_c, cot_y1, cotangent[TOKENS // 2 :])
    )
    cot_yc1 = lax.ppermute(cot_y1, "c", swap)
    cot_y2 = lax.ppermute(late, "y", swap_y)
    third = exchange(states, ZC)
    key_state, cot_yc1 = lax.optimization_barrier((third.reshape(FEATURES, HEAD), cot_yc1))
    place = (core * 2 + odd).astype(jnp.int32).reshape(1)
    attended, own, give_c, give_y, give_yc = call(
        attend_kernel,
        [SMEM] + [VMEM] * 5,
        [shape((TOKENS, FEATURES), BF16)] + [shape((TOKENS, HEAD), BF16)] * 4,
        (place, queries, keys, values, key_state, scale),
        3 * small,
        scratch_shapes=[pltpu.VMEM((HEADS, TOKENS, HEAD), BF16)],
    )
    late_y = lax.optimization_barrier((cot_y2, attended))[0]
    cot_yc2 = lax.ppermute(late_y, "c", swap)
    got_c = lax.ppermute(give_c, "c", swap)
    got_y = lax.ppermute(give_y, "y", swap_y)
    got_yc = lax.ppermute(give_yc, ("y", "c"), [(i, i ^ 3) for i in range(8)])

    held = [
        pltpu.VMEM((MEMBERS, GROUPS, ROWS, FEATURES), BF16),
        pltpu.SemaphoreType.DMA((CHUNKS,)),
    ]
    gradient, local_grads = call(
        gradient_kernel,
        [HBM, HBM, VMEM, VMEM],
        [shape((TOKENS, FEATURES), BF16), shape((FEATURES, HEAD), BF16)],
        (cotangent, weight, queries, scale),
        large,
        limit=58,
        scratch_shapes=held
        + [pltpu.VMEM((TOKENS, MODEL), BF16), pltpu.SemaphoreType.DMA(())],
    )
    got_c, got_y, got_yc, local_grads, cot_yc2 = lax.optimization_barrier(
        (got_c, got_y, got_yc, local_grads, cot_yc2)
    )
    first = exchange(local_grads.reshape(rows_shape), ZC)
    after, total = sums_before([first[i] for i in reversed(range(MEMBERS))])
    inside = jnp.stack(after[::-1])

    width = SHARE + STATE_ROWS
    steps = 4
    terms = pl.pallas_call(
        weight_kernel,
        grid=(steps,),
        in_specs=[pl.BlockSpec((TOKENS, MODEL // steps), lambda i: (0, i))] * 2
        + [pl.BlockSpec((TOKENS // 2, MODEL // steps), lambda i: (0, i))] * 4
        + [pl.BlockSpec((TOKENS, HEAD), lambda i: (0, 0))] * 4,
        out_specs=pl.BlockSpec((GROUPS // steps, width, HEAD), lambda i: (i, 0, 0)),
        out_shape=shape((GROUPS, width, HEAD), BF16),
        compiler_params=pltpu.CompilerParams(vmem_limit_bytes=32 << 20),
        cost_estimate=pl.CostEstimate(flops=large, bytes_accessed=6 << 20, transcendentals=0),
    )(cotangent, cot_c, cot_y1, cot_y2, cot_yc1, cot_yc2, own, got_c, got_y, got_yc)
    terms = terms.at[:, SHARE:, :].set(total.astype(BF16)[None])
    got = exchange(terms, XY)
    local_args = lax.optimization_barrier((queries, keys, values, gradient, key_state, total))[:5]
    query_gradient, kg_local, vg_local = call(
        local_kernel,
        [VMEM] * 5,
        [shape((TOKENS, FEATURES), BF16)] + [shape((TOKENS, FEATURES), F32)] * 2,
        local_args,
        6 * small,
    )
    mixed_args = lax.optimization_barrier((attended, weight, total))[:2]
    mixed = call(
        mixed_kernel,
        [VMEM, HBM],
        [shape((TOKENS, MODEL), BF16)],
        mixed_args,
        large,
        limit=58,
        scratch_shapes=held,
    )
    got = lax.optimization_barrier((got, mixed, query_gradient))[0]
    back = call(
        reduce_kernel,
        [SMEM, VMEM, VMEM],
        [shape((MEMBERS, 2 * ROWS + STATE_ROWS, HEAD), BF16)],
        (group.astype(jnp.int32).reshape(1), got, inside),
        small,
    )
    last = exchange(back, ZC)
    key_gradient, value_gradient, weight_grad = call(
        final_kernel,
        [VMEM] * 5,
        [shape((TOKENS, FEATURES), BF16)] * 2 + [shape((ROWS, FEATURES), F32)],
        (last, keys, values, kg_local, vg_local),
        2 * small,
    )
    return (mixed, query_gradient, key_gradient, value_gradient, weight_grad)


def solution(mesh):
    grid = Mesh(mesh.devices.reshape(4, 4, 8, 2), ("x", "y", "z", "c"))
    spec = P(("x", "y", "z", "c"), None)
    return jax.shard_map(
        body, mesh=grid, in_specs=(spec,) * 5, out_specs=(spec,) * 5, check_vma=False
    )
```

```python
import jax
import jax.numpy as jnp
from jax import lax
from jax.experimental import pallas as pl
from jax.experimental.pallas import tpu as pltpu
from jax.sharding import Mesh, PartitionSpec as P

HEADS = 4
HEAD = 128
TOKENS = 128
FEATURES = HEADS * HEAD
MODEL = 4096
GROUPS = 16
MEMBERS = 16
ROWS = MODEL // (GROUPS * MEMBERS)
SHARE = MODEL // GROUPS
STATE_ROWS = FEATURES // MEMBERS
CHUNKS = 4
LIMIT = 63_000_000
ROOM = 32_000_000
SLICE = HEAD // MEMBERS
FLIPS = (0, 2, 1, 3)
XY = ("x", "y")
ZC = ("z", "c")
BF16 = jnp.bfloat16
F32 = jnp.float32
NN = (((1,), (0,)), ((), ()))
NT = (((1,), (1,)), ((), ()))
TN = (((0,), (0,)), ((), ()))
VMEM = pl.BlockSpec(memory_space=pltpu.VMEM)
SMEM = pl.BlockSpec(memory_space=pltpu.SMEM)
HBM = pl.BlockSpec(memory_space=pltpu.HBM)


def mul(a, b, dims):
    return lax.dot_general(a, b, dims, preferred_element_type=F32)


def shape(dims, dtype):
    return jax.ShapeDtypeStruct(dims, dtype)


def call(kernel, ins, outs, args, flops, limit=LIMIT, **kw):
    out_bytes = sum(o.size * o.dtype.itemsize for o in outs)
    in_bytes = sum(a.size * a.dtype.itemsize for a in args)
    one = len(outs) == 1
    return pl.pallas_call(
        kernel,
        in_specs=ins,
        out_specs=VMEM if one else [VMEM] * len(outs),
        out_shape=outs[0] if one else outs,
        compiler_params=pltpu.CompilerParams(vmem_limit_bytes=limit),
        cost_estimate=pl.CostEstimate(
            flops=flops, bytes_accessed=in_bytes + out_bytes, transcendentals=0
        ),
        **kw,
    )(*args)


def head(ref, h):
    return ref[:, h * HEAD : (h + 1) * HEAD]


def state(ref, h):
    return ref[h * HEAD : (h + 1) * HEAD, :]


def scale_from(first):
    token = first + lax.broadcasted_iota(jnp.int32, (TOKENS, HEAD), 0)
    return lax.rsqrt((HEAD * (token + 1)).astype(F32))


def causal(x):
    row = lax.broadcasted_iota(jnp.int32, x.shape, 0)
    col = lax.broadcasted_iota(jnp.int32, x.shape, 1)
    return jnp.where(row >= col, x, 0.0).astype(BF16)


def keys_kernel(me, k, v, w, q, out, q0, q1, q2, q3):
    for h in range(HEADS):
        product = mul(head(k, h), head(v, h), TN).astype(BF16)
        for i in range(HEAD // STATE_ROWS):
            at = slice(i * STATE_ROWS, (i + 1) * STATE_ROWS)
            out[h * (HEAD // STATE_ROWS) + i, :STATE_ROWS, :] = product[at]
    for m in range(MEMBERS):
        out[m, STATE_ROWS:, :] = head(w, head_of(m))
    for flip, ref in zip(FLIPS, (q0, q1, q2, q3)):
        ref[...] = q[:, head_at(me[0] ^ flip)]


def head_of(m):
    return (m % 2) * 2 + (m % 4) // 2


def head_at(h):
    return pl.ds(pl.multiple_of(h * HEAD, HEAD), HEAD)


def before_kernel(first, inside, send):
    running = jnp.zeros((STATE_ROWS, HEAD), F32)
    rows = []
    for m in range(MEMBERS):
        inside[m] = running
        running = running + first[m, :STATE_ROWS, :].astype(F32)
        rows.append(first[m, STATE_ROWS:, :])
    packed = jnp.concatenate([running.astype(BF16)] + rows, axis=0)
    for j in range(GROUPS):
        send[j] = packed


def carry_kernel(group, second, inside, out):
    carried = jnp.zeros((STATE_ROWS, HEAD), F32)
    for j in range(GROUPS):
        piece = second[j, :STATE_ROWS, :].astype(F32)
        carried = carried + jnp.where(j < group[0], piece, 0.0)
    for m in range(MEMBERS):
        out[m] = (inside[m] + carried).astype(BF16)


def attend_kernel(me, base, q, k, v, key_state, out, a0, a1, a2, a3, by_head):
    scale = scale_from(base[0] + base[1] * TOKENS)
    for h in range(HEADS):
        qh = head(q, h)
        scores = causal(mul(qh, head(k, h), NT))
        total = mul(scores, head(v, h), NN) + mul(qh, state(key_state, h), NN)
        result = (total * scale).astype(BF16)
        out[:, h * HEAD : (h + 1) * HEAD] = result
        by_head[h] = result
    for flip, ref in zip(FLIPS, (a0, a1, a2, a3)):
        ref[...] = by_head[me[0] ^ flip]


def gradient_kernel(base, c0, c1, c2, c3, w, q0, q1, q2, q3, g0, g1, g2, g3, out, total):
    step = pl.program_id(0)
    left = jnp.concatenate([c[...] for c in (c0, c1, c2, c3)], axis=0)
    rows = [w[j, STATE_ROWS:, :] for j in range(GROUPS // CHUNKS)]
    term = mul(left, jnp.concatenate(rows, axis=0), NN)

    @pl.when(step == 0)
    def _():
        total[...] = term

    @pl.when(step > 0)
    def _():
        total[...] += term

    @pl.when(step == CHUNKS - 1)
    def _():
        sums = []
        for i, (q, g) in enumerate(zip((q0, q1, q2, q3), (g0, g1, g2, g3))):
            scale = scale_from(base[0] + (base[1] ^ i) * TOKENS)
            value = (total[i * TOKENS : (i + 1) * TOKENS] * scale).astype(BF16)
            g[...] = value
            sums.append(mul(q[...], value, TN))
        for m in range(MEMBERS):
            at = slice(m * SLICE, (m + 1) * SLICE)
            out[m] = jnp.concatenate([x[at] for x in sums], axis=0).astype(BF16)


def after_kernel(first, inside, total):
    pieces = [first[m].astype(F32) for m in range(MEMBERS)]
    running = jnp.zeros((STATE_ROWS, HEAD), F32)
    for block in reversed(range(MEMBERS)):
        quad, local = block // 4, block % 4
        inside[block] = running
        rows = []
        for h in range(HEADS):
            place = (h % 2) * 2 + h // 2
            at = (place ^ local) * SLICE
            rows.append(pieces[quad * 4 + place][at : at + SLICE])
        running = running + jnp.concatenate(rows, axis=0)
    total[...] = running.astype(BF16)


def mixed_kernel(me, att, w0, w1, w2, w3, out):
    left = jnp.concatenate([att[:, head_at(me[0] ^ flip)] for flip in FLIPS], axis=1)
    for j in range(GROUPS):
        right = jnp.concatenate([w[j, STATE_ROWS:, :] for w in (w0, w1, w2, w3)], axis=1)
        out[:, j * SHARE : (j + 1) * SHARE] = mul(left, right, NT).astype(BF16)


def weight_kernel(c0, c1, c2, c3, a0, a1, a2, a3, out):
    turned = jnp.concatenate([a[...].T for a in (a0, a1, a2, a3)], axis=1)
    for j in range(out.shape[0]):
        at = slice(j * SHARE, (j + 1) * SHARE)
        cots = jnp.concatenate([c[:, at] for c in (c0, c1, c2, c3)], axis=0)
        term = mul(turned, cots, NN).astype(BF16)
        for half in range(2):
            out[j, half * HEAD : (half + 1) * HEAD, :] = term[:, half * HEAD : (half + 1) * HEAD]
        out[j, SHARE:, :] = jnp.zeros((STATE_ROWS, HEAD), BF16)


def local_kernel(me, q, k, v, g0, g1, g2, g3, key_state, qg, kg, vg, by_head):
    for flip, ref in zip(FLIPS, (g0, g1, g2, g3)):
        by_head[me[0] ^ flip] = ref[...]
    for h in range(HEADS):
        at = slice(h * HEAD, (h + 1) * HEAD)
        qh, kh, vh, gh = head(q, h), head(k, h), head(v, h), by_head[h]
        scores = causal(mul(qh, kh, NT))
        grads = causal(mul(gh, vh, NT))
        qg[:, at] = (mul(grads, kh, NN) + mul(gh, state(key_state, h), NT)).astype(BF16)
        kg[:, at] = mul(grads, qh, TN)
        vg[:, at] = mul(scores, gh, TN)


def reduce_kernel(group, got, inside, out):
    after = jnp.zeros((STATE_ROWS, HEAD), F32)
    for j in range(GROUPS):
        piece = got[j, SHARE:, :].astype(F32)
        after = after + jnp.where(j > group[0], piece, 0.0)
    for m in range(MEMBERS):
        out[m, ROWS:, :] = (inside[m] + after).astype(BF16)
    per = HEAD // ROWS
    for half in range(2):
        total = None
        for j in range(GROUPS):
            piece = got[j, half * HEAD : (half + 1) * HEAD, :].astype(F32)
            total = piece if total is None else total + piece
        turned = total.T.astype(BF16)
        for m in range(per):
            out[half * per + m, :ROWS, :] = turned[m * ROWS : (m + 1) * ROWS]


def final_kernel(got, k, v, kg_local, vg_local, kg, vg, wg):
    states = [got[m, ROWS:, :].astype(F32) for m in range(MEMBERS)]
    for h in range(HEADS):
        at = slice(h * HEAD, (h + 1) * HEAD)
        rows = [x[h * SLICE : (h + 1) * SLICE] for x in states]
        grad_state = jnp.concatenate(rows, axis=0).astype(BF16)
        kg[:, at] = (kg_local[:, at] + mul(head(v, h), grad_state, NT)).astype(BF16)
        vg[:, at] = (vg_local[:, at] + mul(head(k, h), grad_state, NN)).astype(BF16)
        total = None
        for quad in range(MEMBERS // 4):
            piece = got[quad * 4 + (h % 2) * 2 + h // 2, :ROWS, :].astype(F32)
            total = piece if total is None else total + piece
        wg[:, at] = total


def exchange(value, axes):
    return lax.all_to_all(value, axes, 0, 0, tiled=True)


def body(queries, keys, values, out_weight, cotangent):
    group = lax.axis_index(XY).astype(jnp.int32)
    member = lax.axis_index(ZC)
    core = lax.axis_index("c")
    odd = lax.rem(lax.axis_index("z"), 2)
    me = (core * 2 + odd).astype(jnp.int32).reshape(1)
    group_id = group.reshape(1)

    base = jnp.stack([group * MEMBERS * TOKENS, member.astype(jnp.int32)])

    def to_core(x):
        return lax.ppermute(x, "c", [(0, 1), (1, 0)])

    def to_odd(x):
        return lax.ppermute(x, "z", [(i, i ^ 1) for i in range(8)])

    def to_both(x):
        return lax.ppermute(x, ZC, [(i, i ^ 3) for i in range(MEMBERS)])

    head_block = shape((TOKENS, HEAD), BF16)
    small = 2 * TOKENS * HEAD * FEATURES
    large = 2 * TOKENS * MODEL * FEATURES
    by_head = [pltpu.VMEM((HEADS, TOKENS, HEAD), BF16)]

    sent, q0, q1, q2, q3 = call(
        keys_kernel,
        [SMEM] + [VMEM] * 4,
        [shape((MEMBERS, STATE_ROWS + ROWS, HEAD), BF16)] + [head_block] * 4,
        (me, keys, values, out_weight, queries),
        small,
    )
    first = exchange(sent, ZC)
    cot_c = to_core(cotangent)
    q1, q2, q3 = to_core(q1), to_odd(q2), to_both(q3)
    inside, sent = call(
        before_kernel,
        [VMEM],
        [
            shape((MEMBERS, STATE_ROWS, HEAD), F32),
            shape((GROUPS, STATE_ROWS + SHARE, HEAD), BF16),
        ],
        (first,),
        small,
        limit=ROOM,
    )
    sent, cot_c, q1, q2, q3, late = lax.optimization_barrier((sent, cot_c, q1, q2, q3, cotangent))
    cot_z = to_odd(late)
    second = exchange(sent, XY)
    cot_zc = to_core(cot_z)
    states = call(
        carry_kernel,
        [SMEM, VMEM, VMEM],
        [shape((MEMBERS, STATE_ROWS, HEAD), BF16)],
        (group_id, second, inside),
        small,
        limit=ROOM,
    )
    third = exchange(states, ZC)
    key_state = third.reshape(FEATURES, HEAD)
    wide = pl.BlockSpec((TOKENS, MODEL // CHUNKS), lambda i: (0, i))
    whole = pl.BlockSpec((TOKENS, HEAD), lambda i: (0, 0))
    g0, g1, g2, g3, sent = pl.pallas_call(
        gradient_kernel,
        grid=(CHUNKS,),
        in_specs=[SMEM]
        + [wide] * 4
        + [pl.BlockSpec((GROUPS // CHUNKS, STATE_ROWS + SHARE, HEAD), lambda i: (i, 0, 0))]
        + [whole] * 4,
        out_specs=[whole] * 4
        + [pl.BlockSpec((MEMBERS, STATE_ROWS, HEAD), lambda i: (0, 0, 0))],
        out_shape=[head_block] * 4 + [shape((MEMBERS, STATE_ROWS, HEAD), BF16)],
        scratch_shapes=[pltpu.VMEM((4 * TOKENS, HEAD), F32)],
        compiler_params=pltpu.CompilerParams(vmem_limit_bytes=LIMIT),
        cost_estimate=pl.CostEstimate(flops=large, bytes_accessed=6 << 20, transcendentals=0),
    )(base, cotangent, cot_c, cot_z, cot_zc, second, q0, q1, q2, q3)
    key_state, sent, g0 = lax.optimization_barrier((key_state, sent, g0))
    attended, a0, a1, a2, a3 = call(
        attend_kernel,
        [SMEM] * 2 + [VMEM] * 4,
        [shape((TOKENS, FEATURES), BF16)] + [head_block] * 4,
        (me, base, queries, keys, values, key_state),
        3 * small,
        scratch_shapes=by_head,
    )
    a1, a2, a3 = to_core(a1), to_odd(a2), to_both(a3)
    g1, g2, g3 = to_core(g1), to_odd(g2), to_both(g3)
    fourth = exchange(sent, ZC)
    width = SHARE + STATE_ROWS
    terms = pl.pallas_call(
        weight_kernel,
        grid=(CHUNKS,),
        in_specs=[wide] * 4 + [whole] * 4,
        out_specs=pl.BlockSpec((GROUPS // CHUNKS, width, HEAD), lambda i: (i, 0, 0)),
        out_shape=shape((GROUPS, width, HEAD), BF16),
        compiler_params=pltpu.CompilerParams(vmem_limit_bytes=LIMIT),
        cost_estimate=pl.CostEstimate(flops=large, bytes_accessed=6 << 20, transcendentals=0),
    )(cotangent, cot_c, cot_z, cot_zc, a0, a1, a2, a3)
    fourth, terms, g1, g2, g3 = lax.optimization_barrier((fourth, terms, g1, g2, g3))
    inside, total = call(
        after_kernel,
        [VMEM],
        [shape((MEMBERS, STATE_ROWS, HEAD), F32), shape((STATE_ROWS, HEAD), BF16)],
        (fourth,),
        small,
        limit=ROOM,
    )
    terms = terms.at[:, SHARE:, :].set(total[None])
    got = exchange(terms, XY)

    w0, g0, attended = lax.optimization_barrier((second, g0, attended, total, a1, a2, a3))[:3]
    w1, w2 = to_core(w0), to_odd(w0)
    query_gradient, kg_local, vg_local = call(
        local_kernel,
        [SMEM] + [VMEM] * 8,
        [shape((TOKENS, FEATURES), BF16)] + [shape((TOKENS, FEATURES), F32)] * 2,
        (me, queries, keys, values, g0, g1, g2, g3, key_state),
        6 * small,
        scratch_shapes=by_head,
    )
    got = lax.optimization_barrier((got, query_gradient))[0]
    back = call(
        reduce_kernel,
        [SMEM, VMEM, VMEM],
        [shape((MEMBERS, ROWS + STATE_ROWS, HEAD), BF16)],
        (group_id, got, inside),
        small,
        limit=ROOM,
    )
    back, w2 = lax.optimization_barrier((back, w2))
    w3 = to_core(w2)
    last = exchange(back, ZC)
    mixed = call(
        mixed_kernel,
        [SMEM] + [VMEM] * 5,
        [shape((TOKENS, MODEL), BF16)],
        (me, attended, w0, w1, w2, w3),
        large,
    )
    last, mixed = lax.optimization_barrier((last, mixed))
    key_gradient, value_gradient, weight_grad = call(
        final_kernel,
        [VMEM] * 5,
        [shape((TOKENS, FEATURES), BF16)] * 2 + [shape((ROWS, FEATURES), F32)],
        (last, keys, values, kg_local, vg_local),
        2 * small,
        limit=ROOM,
    )
    return (mixed, query_gradient, key_gradient, value_gradient, weight_grad)


def solution(mesh):
    grid = Mesh(mesh.devices.reshape(4, 4, 8, 2), ("x", "y", "z", "c"))
    spec = P(("x", "y", "z", "c"), None)
    return jax.shard_map(
        body, mesh=grid, in_specs=(spec,) * 5, out_specs=(spec,) * 5, check_vma=False
    )
```

```python
import jax
import jax.numpy as jnp
from jax import lax
from jax.experimental import pallas as pl
from jax.experimental.pallas import tpu as pltpu
from jax.sharding import Mesh, PartitionSpec as P

HEADS = 4
HEAD = 128
TOKENS = 128
FEATURES = HEADS * HEAD
MODEL = 4096
GROUPS = 16
MEMBERS = 16
ROWS = MODEL // (GROUPS * MEMBERS)
SHARE = MODEL // GROUPS
STATE_ROWS = FEATURES // MEMBERS
CHUNKS = 4
LIMIT = 63_000_000
SOME = 60_000_000
ROOM = 32_000_000
SLICE = HEAD // MEMBERS
FLIPS = (0, 2, 1, 3)
XY = ("x", "y")
ZC = ("z", "c")
BF16 = jnp.bfloat16
F32 = jnp.float32
NN = (((1,), (0,)), ((), ()))
NT = (((1,), (1,)), ((), ()))
TN = (((0,), (0,)), ((), ()))
VMEM = pl.BlockSpec(memory_space=pltpu.VMEM)
SMEM = pl.BlockSpec(memory_space=pltpu.SMEM)
HBM = pl.BlockSpec(memory_space=pl.ANY)


def mul(a, b, dims):
    return lax.dot_general(a, b, dims, preferred_element_type=F32)


def shape(dims, dtype):
    return jax.ShapeDtypeStruct(dims, dtype)


def call(kernel, ins, outs, args, flops, limit=LIMIT, **kw):
    out_bytes = sum(o.size * o.dtype.itemsize for o in outs)
    in_bytes = sum(a.size * a.dtype.itemsize for a in args)
    one = len(outs) == 1
    return pl.pallas_call(
        kernel,
        in_specs=ins,
        out_specs=VMEM if one else [VMEM] * len(outs),
        out_shape=outs[0] if one else outs,
        compiler_params=pltpu.CompilerParams(vmem_limit_bytes=limit),
        cost_estimate=pl.CostEstimate(
            flops=flops, bytes_accessed=in_bytes + out_bytes, transcendentals=0
        ),
        **kw,
    )(*args)


def head(ref, h):
    return ref[:, h * HEAD : (h + 1) * HEAD]


def scale_from(first):
    token = first + lax.broadcasted_iota(jnp.int32, (TOKENS, HEAD), 0)
    return lax.rsqrt((HEAD * (token + 1)).astype(F32))


def causal(x):
    row = lax.broadcasted_iota(jnp.int32, x.shape, 0)
    col = lax.broadcasted_iota(jnp.int32, x.shape, 1)
    return jnp.where(row >= col, x, 0.0).astype(BF16)


def keys_kernel(me, k, v, w, q, out, x0, x1, x2, x3):
    products = [mul(head(k, h), head(v, h), TN) for h in range(HEADS)]
    for m in range(MEMBERS):
        rows = [x[m * SLICE : (m + 1) * SLICE] for x in products]
        out[m, :STATE_ROWS, :] = jnp.concatenate(rows, axis=0).astype(BF16)
        out[m, STATE_ROWS:, :] = head(w, head_of(m))
    for flip, ref in zip(FLIPS, (x0, x1, x2, x3)):
        at = head_at(me[0] ^ flip)
        for i, x in enumerate((q, k, v)):
            ref[i * TOKENS : (i + 1) * TOKENS, :] = x[:, at]


def head_of(m):
    return (m % 2) * 2 + (m % 4) // 2


def head_at(h):
    return pl.ds(pl.multiple_of(h * HEAD, HEAD), HEAD)


def before_kernel(first, inside, send):
    running = jnp.zeros((STATE_ROWS, HEAD), F32)
    rows = []
    for m in range(MEMBERS):
        inside[m] = running
        running = running + first[m, :STATE_ROWS, :].astype(F32)
        rows.append(first[m, STATE_ROWS:, :])
    packed = jnp.concatenate([running.astype(BF16)] + rows, axis=0)
    for j in range(GROUPS):
        send[j] = packed


def carry_kernel(group, second, inside, out):
    carried = jnp.zeros((STATE_ROWS, HEAD), F32)
    for j in range(GROUPS):
        piece = second[j, :STATE_ROWS, :].astype(F32)
        carried = carried + jnp.where(j < group[0], piece, 0.0)
    states = [inside[m] + carried for m in range(MEMBERS)]
    for m in range(MEMBERS):
        at = head_of(m) * SLICE
        rows = [states[m ^ k][at : at + SLICE] for k in range(4)]
        out[m] = jnp.concatenate(rows, axis=0).astype(BF16)


def attend_kernel(
    base, place, x0, x1, x2, x3, got, g1, g2, g3, a0, a1, a2, a3, s0, p1, p2, p3
):
    slices = [got[m].astype(F32) for m in range(MEMBERS)]
    for i, (x, a) in enumerate(zip((x0, x1, x2, x3), (a0, a1, a2, a3))):
        rows = [piece[i * SLICE : (i + 1) * SLICE] for piece in slices]
        key_state = jnp.concatenate(rows, axis=0).astype(BF16)
        q, k, v = (x[j * TOKENS : (j + 1) * TOKENS, :] for j in range(3))
        scores = causal(mul(q, k, NT))
        total = mul(scores, v, NN) + mul(q, key_state, NN)
        result = (total * scale_from(base[0] + (place[0] ^ i) * TOKENS)).astype(BF16)
        a[...] = result
        if i == 0:
            s0[...] = key_state
        else:
            pair, g = ((p1, g1), (p2, g2), (p3, g3))[i - 1]
            pair[:TOKENS] = result
            pair[TOKENS : 2 * TOKENS] = g[...]
            pair[2 * TOKENS :] = key_state


def gradient_kernel(
    base, place, c0, c1, c2, c3, w, x0, x1, x2, x3, g0, g1, g2, g3, out, cots, held, sems
):
    copies = [
        pltpu.make_async_copy(c, cots.at[i], sems.at[i]) for i, c in enumerate((c0, c1, c2, c3))
    ]
    weight_copy = pltpu.make_async_copy(w, held, sems.at[4])
    weight_copy.start()
    for copy in copies:
        copy.start()
    weight_copy.wait()
    right = held[:, STATE_ROWS:, :].reshape(MODEL, HEAD)
    sums = []
    for i, (x, g) in enumerate(zip((x0, x1, x2, x3), (g0, g1, g2, g3))):
        copies[i].wait()
        scale = scale_from(base[0] + (place[0] ^ i) * TOKENS)
        total = mul(cots[i], right, NN)
        value = (total * scale).astype(BF16)
        g[...] = value
        sums.append(mul(x[:TOKENS, :], value, TN))
    for m in range(MEMBERS):
        at = slice(m * SLICE, (m + 1) * SLICE)
        out[m] = jnp.concatenate([x[at] for x in sums], axis=0).astype(BF16)


def after_kernel(first, inside, total):
    pieces = [first[m].astype(F32) for m in range(MEMBERS)]
    running = jnp.zeros((STATE_ROWS, HEAD), F32)
    for block in reversed(range(MEMBERS)):
        quad, local = block // 4, block % 4
        inside[block] = running
        rows = []
        for h in range(HEADS):
            place = (h % 2) * 2 + h // 2
            at = (place ^ local) * SLICE
            rows.append(pieces[quad * 4 + place][at : at + SLICE])
        running = running + jnp.concatenate(rows, axis=0)
    total[...] = running.astype(BF16)


def mixed_kernel(a0, p1, p2, p3, *refs):
    *parts, out = refs
    left = jnp.concatenate([a0[...]] + [p[:TOKENS] for p in (p1, p2, p3)], axis=1)
    for j in range(GROUPS):
        half, at = divmod(j, GROUPS // 2)
        right = jnp.concatenate([w[at] for w in parts[half::2]], axis=1)
        out[:, j * SHARE : (j + 1) * SHARE] = mul(left, right, NT).astype(BF16)


def weight_kernel(c0, c1, c2, c3, a0, a1, a2, a3, out, cots, sems):
    width = MODEL // CHUNKS
    copies = []
    for step in range(CHUNKS):
        at = pl.ds(step * width, width)
        copies.append(
            [
                pltpu.make_async_copy(c.at[:, at], cots.at[i, :, at], sems.at[step, i])
                for i, c in enumerate((c0, c1, c2, c3))
            ]
        )
    for group in copies:
        for copy in group:
            copy.start()
    turned = jnp.concatenate([a[...].T for a in (a0, a1, a2, a3)], axis=1)
    for j in range(GROUPS):
        if j % (GROUPS // CHUNKS) == 0:
            for copy in copies[j // (GROUPS // CHUNKS)]:
                copy.wait()
        at = slice(j * SHARE, (j + 1) * SHARE)
        right = cots[:, :, at].reshape(4 * TOKENS, SHARE)
        term = mul(turned, right, NN).astype(BF16)
        for half in range(2):
            out[j, half * HEAD : (half + 1) * HEAD, :] = term[:, half * HEAD : (half + 1) * HEAD]
        out[j, SHARE:, :] = jnp.zeros((STATE_ROWS, HEAD), BF16)


def local_kernel(me, q, k, v, g0, s0, p1, p2, p3, qg, kg, vg, by_head):
    by_head[me[0], :TOKENS] = g0[...]
    by_head[me[0], TOKENS:] = s0[...]
    for flip, pair in zip(FLIPS[1:], (p1, p2, p3)):
        by_head[me[0] ^ flip] = pair[TOKENS:]
    for h in range(HEADS):
        at = slice(h * HEAD, (h + 1) * HEAD)
        qh, kh, vh, gh = head(q, h), head(k, h), head(v, h), by_head[h, :TOKENS]
        scores = causal(mul(qh, kh, NT))
        grads = causal(mul(gh, vh, NT))
        qg[:, at] = (mul(grads, kh, NN) + mul(gh, by_head[h, TOKENS:], NT)).astype(BF16)
        kg[:, at] = mul(grads, qh, TN)
        vg[:, at] = mul(scores, gh, TN)


def reduce_kernel(group, got, inside, out):
    after = jnp.zeros((STATE_ROWS, HEAD), F32)
    for j in range(GROUPS):
        piece = got[j, SHARE:, :].astype(F32)
        after = after + jnp.where(j > group[0], piece, 0.0)
    for m in range(MEMBERS):
        out[m, ROWS:, :] = (inside[m] + after).astype(BF16)
    per = HEAD // ROWS
    for half in range(2):
        total = None
        for j in range(GROUPS):
            piece = got[j, half * HEAD : (half + 1) * HEAD, :].astype(F32)
            total = piece if total is None else total + piece
        turned = total.T.astype(BF16)
        for m in range(per):
            out[half * per + m, :ROWS, :] = turned[m * ROWS : (m + 1) * ROWS]


def final_kernel(got, k, v, kg_local, vg_local, kg, vg, wg):
    states = [got[m, ROWS:, :].astype(F32) for m in range(MEMBERS)]
    for h in range(HEADS):
        at = slice(h * HEAD, (h + 1) * HEAD)
        rows = [x[h * SLICE : (h + 1) * SLICE] for x in states]
        grad_state = jnp.concatenate(rows, axis=0).astype(BF16)
        kg[:, at] = (kg_local[:, at] + mul(head(v, h), grad_state, NT)).astype(BF16)
        vg[:, at] = (vg_local[:, at] + mul(head(k, h), grad_state, NN)).astype(BF16)
        total = None
        for quad in range(MEMBERS // 4):
            piece = got[quad * 4 + (h % 2) * 2 + h // 2, :ROWS, :].astype(F32)
            total = piece if total is None else total + piece
        wg[:, at] = total


def exchange(value, axes):
    return lax.all_to_all(value, axes, 0, 0, tiled=True)


def body(queries, keys, values, out_weight, cotangent):
    group = lax.axis_index(XY).astype(jnp.int32)
    member = lax.axis_index(ZC)
    core = lax.axis_index("c")
    odd = lax.rem(lax.axis_index("z"), 2)
    me = (core * 2 + odd).astype(jnp.int32).reshape(1)
    group_id = group.reshape(1)

    base = (group * MEMBERS * TOKENS).reshape(1)
    place = member.astype(jnp.int32).reshape(1)

    def to_core(x):
        return lax.ppermute(x, "c", [(0, 1), (1, 0)])

    def to_odd(x):
        return lax.ppermute(x, "z", [(i, i ^ 1) for i in range(8)])

    def to_both(x):
        return lax.ppermute(x, ZC, [(i, i ^ 3) for i in range(MEMBERS)])

    head_block = shape((TOKENS, HEAD), BF16)
    small = 2 * TOKENS * HEAD * FEATURES
    large = 2 * TOKENS * MODEL * FEATURES
    triple = shape((3 * TOKENS, HEAD), BF16)

    sent, x0, x1, x2, x3 = call(
        keys_kernel,
        [SMEM] + [VMEM] * 4,
        [shape((MEMBERS, STATE_ROWS + ROWS, HEAD), BF16)] + [triple] * 4,
        (me, keys, values, out_weight, queries),
        small,
    )
    first = exchange(sent, ZC)
    cot_c = to_core(cotangent)
    x1, x2, x3 = to_core(x1), to_odd(x2), to_both(x3)
    inside, sent = call(
        before_kernel,
        [VMEM],
        [
            shape((MEMBERS, STATE_ROWS, HEAD), F32),
            shape((GROUPS, STATE_ROWS + SHARE, HEAD), BF16),
        ],
        (first,),
        small,
        limit=ROOM,
    )
    sent, cot_c, x1, x2, x3, late = lax.optimization_barrier((sent, cot_c, x1, x2, x3, cotangent))
    cot_z = to_odd(late)
    second = exchange(sent, XY)
    cot_zc = to_core(cot_z)
    states = call(
        carry_kernel,
        [SMEM, VMEM, VMEM],
        [shape((MEMBERS, STATE_ROWS, HEAD), BF16)],
        (group_id, second, inside),
        small,
        limit=ROOM,
    )
    third = exchange(states, ZC)
    g0, g1, g2, g3, sent = call(
        gradient_kernel,
        [SMEM] * 2 + [HBM] * 5 + [VMEM] * 4,
        [head_block] * 4
        + [shape((MEMBERS, STATE_ROWS, HEAD), BF16)],
        (base, place, cotangent, cot_c, cot_z, cot_zc, second, x0, x1, x2, x3),
        large,
        scratch_shapes=[
            pltpu.VMEM((4, TOKENS, MODEL), BF16),
            pltpu.VMEM((GROUPS, STATE_ROWS + SHARE, HEAD), BF16),
            pltpu.SemaphoreType.DMA((5,)),
        ],
    )
    third, sent, g0 = lax.optimization_barrier((third, sent, g0))
    a0, a1, a2, a3, s0, p1, p2, p3 = call(
        attend_kernel,
        [SMEM] * 2 + [VMEM] * 8,
        [head_block] * 5 + [triple] * 3,
        (base, place, x0, x1, x2, x3, third, g1, g2, g3),
        3 * small,
    )
    fourth = exchange(sent, ZC)
    width = SHARE + STATE_ROWS
    terms = call(
        weight_kernel,
        [HBM] * 4 + [VMEM] * 4,
        [shape((GROUPS, width, HEAD), BF16)],
        (cotangent, cot_c, cot_z, cot_zc, a0, a1, a2, a3),
        large,
        limit=SOME,
        scratch_shapes=[
            pltpu.VMEM((4, TOKENS, MODEL), BF16),
            pltpu.SemaphoreType.DMA((CHUNKS, 4)),
        ],
    )
    fourth, terms = lax.optimization_barrier((fourth, terms))
    inside, total = call(
        after_kernel,
        [VMEM],
        [shape((MEMBERS, STATE_ROWS, HEAD), F32), shape((STATE_ROWS, HEAD), BF16)],
        (fourth,),
        small,
        limit=ROOM,
    )
    terms = terms.at[:, SHARE:, :].set(total[None])
    got = exchange(terms, XY)

    p1, p2, p3, weight, _ = lax.optimization_barrier((p1, p2, p3, second, total))
    w0 = [weight[: GROUPS // 2, STATE_ROWS:], weight[GROUPS // 2 :, STATE_ROWS:]]
    p1, p2, p3 = to_core(p1), to_odd(p2), to_both(p3)
    w1 = [to_core(w) for w in w0]
    ring = [(i, (i + 1) % 8) for i in range(8)]
    w2 = [lax.ppermute(w0[0], "z", ring), lax.ppermute(w0[1], "z", [(j, i) for i, j in ring])]
    got, w1 = lax.optimization_barrier((got, w1))
    back = call(
        reduce_kernel,
        [SMEM, VMEM, VMEM],
        [shape((MEMBERS, ROWS + STATE_ROWS, HEAD), BF16)],
        (group_id, got, inside),
        small,
        limit=ROOM,
    )
    back, w2, p1, p2, p3 = lax.optimization_barrier((back, w2, p1, p2, p3))
    w3 = [to_core(w) for w in w2]
    last = exchange(back, ZC)
    mixed = call(
        mixed_kernel,
        [VMEM] * 12,
        [shape((TOKENS, MODEL), BF16)],
        (a0, p1, p2, p3, *w0, *w1, *w2, *w3),
        large,
    )
    query_gradient, kg_local, vg_local = call(
        local_kernel,
        [SMEM] + [VMEM] * 8,
        [shape((TOKENS, FEATURES), BF16)] + [shape((TOKENS, FEATURES), F32)] * 2,
        (me, queries, keys, values, g0, s0, p1, p2, p3),
        6 * small,
        scratch_shapes=[pltpu.VMEM((HEADS, 2 * TOKENS, HEAD), BF16)],
    )
    last, mixed, kg_local = lax.optimization_barrier((last, mixed, kg_local))
    key_gradient, value_gradient, weight_grad = call(
        final_kernel,
        [VMEM] * 5,
        [shape((TOKENS, FEATURES), BF16)] * 2 + [shape((ROWS, FEATURES), F32)],
        (last, keys, values, kg_local, vg_local),
        2 * small,
        limit=ROOM,
    )
    return (mixed, query_gradient, key_gradient, value_gradient, weight_grad)


def solution(mesh):
    grid = Mesh(mesh.devices.reshape(4, 4, 8, 2), ("x", "y", "z", "c"))
    spec = P(("x", "y", "z", "c"), None)
    return jax.shard_map(
        body, mesh=grid, in_specs=(spec,) * 5, out_specs=(spec,) * 5, check_vma=False
    )
```

```python
import jax
import jax.numpy as jnp
from jax import lax
from jax.experimental import pallas as pl
from jax.experimental.pallas import tpu as pltpu
from jax.sharding import Mesh, PartitionSpec as P

HEADS = 4
HEAD = 128
TOKENS = 128
FEATURES = HEADS * HEAD
MODEL = 4096
GROUPS = 16
MEMBERS = 16
ROWS = MODEL // (GROUPS * MEMBERS)
SHARE = MODEL // GROUPS
STATE_ROWS = FEATURES // MEMBERS
CHUNKS = 4
LIMIT = 63_000_000
SOME = 60_000_000
ROOM = 32_000_000
SLICE = HEAD // MEMBERS
FLIPS = (0, 2, 1, 3)
XY = ("x", "y")
ZC = ("z", "c")
BF16 = jnp.bfloat16
F32 = jnp.float32
NN = (((1,), (0,)), ((), ()))
NT = (((1,), (1,)), ((), ()))
TN = (((0,), (0,)), ((), ()))
VMEM = pl.BlockSpec(memory_space=pltpu.VMEM)
SMEM = pl.BlockSpec(memory_space=pltpu.SMEM)
HBM = pl.BlockSpec(memory_space=pl.ANY)


def mul(a, b, dims):
    return lax.dot_general(a, b, dims, preferred_element_type=F32)


def shape(dims, dtype):
    return jax.ShapeDtypeStruct(dims, dtype)


def call(kernel, ins, outs, args, flops, limit=LIMIT, **kw):
    out_bytes = sum(o.size * o.dtype.itemsize for o in outs)
    in_bytes = sum(a.size * a.dtype.itemsize for a in args)
    one = len(outs) == 1
    return pl.pallas_call(
        kernel,
        in_specs=ins,
        out_specs=VMEM if one else [VMEM] * len(outs),
        out_shape=outs[0] if one else outs,
        compiler_params=pltpu.CompilerParams(vmem_limit_bytes=limit),
        cost_estimate=pl.CostEstimate(
            flops=flops, bytes_accessed=in_bytes + out_bytes, transcendentals=0
        ),
        **kw,
    )(*args)


def head(ref, h):
    return ref[:, h * HEAD : (h + 1) * HEAD]


def scale_from(first):
    token = first + lax.broadcasted_iota(jnp.int32, (TOKENS, HEAD), 0)
    return lax.rsqrt((HEAD * (token + 1)).astype(F32))


def causal(x):
    row = lax.broadcasted_iota(jnp.int32, x.shape, 0)
    col = lax.broadcasted_iota(jnp.int32, x.shape, 1)
    return jnp.where(row >= col, x, 0.0).astype(BF16)


def keys_kernel(me, k, v, w, q, out, x0, x1, x2, x3):
    products = [mul(head(k, h), head(v, h), TN) for h in range(HEADS)]
    for m in range(MEMBERS):
        rows = [x[m * SLICE : (m + 1) * SLICE] for x in products]
        out[m, :STATE_ROWS, :] = jnp.concatenate(rows, axis=0).astype(BF16)
        out[m, STATE_ROWS:, :] = head(w, head_of(m))
    for flip, ref in zip(FLIPS, (x0, x1, x2, x3)):
        at = head_at(me[0] ^ flip)
        for i, x in enumerate((q, k, v)):
            ref[i * TOKENS : (i + 1) * TOKENS, :] = x[:, at]


def head_of(m):
    return (m % 2) * 2 + (m % 4) // 2


def head_at(h):
    return pl.ds(pl.multiple_of(h * HEAD, HEAD), HEAD)


def before_kernel(first, inside, send):
    running = jnp.zeros((STATE_ROWS, HEAD), F32)
    rows = []
    for m in range(MEMBERS):
        inside[m] = running
        running = running + first[m, :STATE_ROWS, :].astype(F32)
        rows.append(first[m, STATE_ROWS:, :])
    packed = jnp.concatenate([running.astype(BF16)] + rows, axis=0)
    for j in range(GROUPS):
        send[j] = packed


def carry_kernel(group, second, inside, out):
    carried = jnp.zeros((STATE_ROWS, HEAD), F32)
    for j in range(GROUPS):
        piece = second[j, :STATE_ROWS, :].astype(F32)
        carried = carried + jnp.where(j < group[0], piece, 0.0)
    states = [inside[m] + carried for m in range(MEMBERS)]
    for m in range(MEMBERS):
        at = head_of(m) * SLICE
        rows = [states[m ^ k][at : at + SLICE] for k in range(4)]
        out[m] = jnp.concatenate(rows, axis=0).astype(BF16)


def attend_kernel(
    base, place, x0, x1, x2, x3, got, g1, g2, g3, a0, a1, a2, a3, s0, p1, p2, p3
):
    slices = [got[m].astype(F32) for m in range(MEMBERS)]
    for i, (x, a) in enumerate(zip((x0, x1, x2, x3), (a0, a1, a2, a3))):
        rows = [piece[i * SLICE : (i + 1) * SLICE] for piece in slices]
        key_state = jnp.concatenate(rows, axis=0).astype(BF16)
        q, k, v = (x[j * TOKENS : (j + 1) * TOKENS, :] for j in range(3))
        scores = causal(mul(q, k, NT))
        total = mul(scores, v, NN) + mul(q, key_state, NN)
        result = (total * scale_from(base[0] + (place[0] ^ i) * TOKENS)).astype(BF16)
        a[...] = result
        if i == 0:
            s0[...] = key_state
        else:
            pair, g = ((p1, g1), (p2, g2), (p3, g3))[i - 1]
            pair[:TOKENS] = result
            pair[TOKENS : 2 * TOKENS] = g[...]
            pair[2 * TOKENS :] = key_state


def gradient_kernel(
    base, place, c0, c1, c2, c3, w, x0, x1, x2, x3, g0, g1, g2, g3, out, cots, held, sems
):
    copies = [
        pltpu.make_async_copy(c, cots.at[i], sems.at[i]) for i, c in enumerate((c0, c1, c2, c3))
    ]
    weight_copy = pltpu.make_async_copy(w, held, sems.at[4])
    weight_copy.start()
    for copy in copies:
        copy.start()
    weight_copy.wait()
    right = held[:, STATE_ROWS:, :].reshape(MODEL, HEAD)
    sums = []
    for i, (x, g) in enumerate(zip((x0, x1, x2, x3), (g0, g1, g2, g3))):
        copies[i].wait()
        scale = scale_from(base[0] + (place[0] ^ i) * TOKENS)
        total = mul(cots[i], right, NN)
        value = (total * scale).astype(BF16)
        g[...] = value
        sums.append(mul(x[:TOKENS, :], value, TN))
    for m in range(MEMBERS):
        at = slice(m * SLICE, (m + 1) * SLICE)
        out[m] = jnp.concatenate([x[at] for x in sums], axis=0).astype(BF16)


def after_kernel(first, inside, total):
    pieces = [first[m].astype(F32) for m in range(MEMBERS)]
    running = jnp.zeros((STATE_ROWS, HEAD), F32)
    for block in reversed(range(MEMBERS)):
        quad, local = block // 4, block % 4
        inside[block] = running
        rows = []
        for h in range(HEADS):
            place = (h % 2) * 2 + h // 2
            at = (place ^ local) * SLICE
            rows.append(pieces[quad * 4 + place][at : at + SLICE])
        running = running + jnp.concatenate(rows, axis=0)
    total[...] = running.astype(BF16)


def mixed_kernel(a0, p1, p2, p3, *refs):
    *parts, out = refs
    left = jnp.concatenate([a0[...]] + [p[:TOKENS] for p in (p1, p2, p3)], axis=1)
    for j in range(GROUPS):
        half, at = divmod(j, GROUPS // 2)
        right = jnp.concatenate([w[at] for w in parts[half::2]], axis=1)
        out[:, j * SHARE : (j + 1) * SHARE] = mul(left, right, NT).astype(BF16)


def weight_kernel(c0, c1, c2, c3, a0, a1, a2, a3, out, cots, result, sems, out_sems):
    width = MODEL // CHUNKS
    part = GROUPS // CHUNKS
    copies = []
    for step in range(CHUNKS):
        at = pl.ds(step * width, width)
        copies.append(
            [
                pltpu.make_async_copy(c.at[:, at], cots.at[i, :, at], sems.at[step, i])
                for i, c in enumerate((c0, c1, c2, c3))
            ]
        )
    for group in copies:
        for copy in group:
            copy.start()
    turned = jnp.concatenate([a[...].T for a in (a0, a1, a2, a3)], axis=1)
    backs = []
    for step in range(CHUNKS):
        for copy in copies[step]:
            copy.wait()
        for j in range(step * part, (step + 1) * part):
            at = slice(j * SHARE, (j + 1) * SHARE)
            right = cots[:, :, at].reshape(4 * TOKENS, SHARE)
            term = mul(turned, right, NN).astype(BF16)
            for half in range(2):
                result[j, half * HEAD : (half + 1) * HEAD, :] = term[
                    :, half * HEAD : (half + 1) * HEAD
                ]
            result[j, SHARE:, :] = jnp.zeros((STATE_ROWS, HEAD), BF16)
        at = pl.ds(step * part, part)
        backs.append(pltpu.make_async_copy(result.at[at], out.at[at], out_sems.at[step]))
        backs[-1].start()
    for back in backs:
        back.wait()


def local_kernel(me, q, k, v, g0, s0, p1, p2, p3, qg, kg, vg, by_head):
    by_head[me[0], :TOKENS] = g0[...]
    by_head[me[0], TOKENS:] = s0[...]
    for flip, pair in zip(FLIPS[1:], (p1, p2, p3)):
        by_head[me[0] ^ flip] = pair[TOKENS:]
    for h in range(HEADS):
        at = slice(h * HEAD, (h + 1) * HEAD)
        qh, kh, vh, gh = head(q, h), head(k, h), head(v, h), by_head[h, :TOKENS]
        scores = causal(mul(qh, kh, NT))
        grads = causal(mul(gh, vh, NT))
        qg[:, at] = (mul(grads, kh, NN) + mul(gh, by_head[h, TOKENS:], NT)).astype(BF16)
        kg[:, at] = mul(grads, qh, TN)
        vg[:, at] = mul(scores, gh, TN)


def reduce_kernel(group, got, inside, out):
    after = jnp.zeros((STATE_ROWS, HEAD), F32)
    for j in range(GROUPS):
        piece = got[j, SHARE:, :].astype(F32)
        after = after + jnp.where(j > group[0], piece, 0.0)
    for m in range(MEMBERS):
        out[m, ROWS:, :] = (inside[m] + after).astype(BF16)
    per = HEAD // ROWS
    for half in range(2):
        total = None
        for j in range(GROUPS):
            piece = got[j, half * HEAD : (half + 1) * HEAD, :].astype(F32)
            total = piece if total is None else total + piece
        turned = total.T.astype(BF16)
        for m in range(per):
            out[half * per + m, :ROWS, :] = turned[m * ROWS : (m + 1) * ROWS]


def final_kernel(got, k, v, kg_local, vg_local, kg, vg, wg):
    states = [got[m, ROWS:, :].astype(F32) for m in range(MEMBERS)]
    for h in range(HEADS):
        at = slice(h * HEAD, (h + 1) * HEAD)
        rows = [x[h * SLICE : (h + 1) * SLICE] for x in states]
        grad_state = jnp.concatenate(rows, axis=0).astype(BF16)
        kg[:, at] = (kg_local[:, at] + mul(head(v, h), grad_state, NT)).astype(BF16)
        vg[:, at] = (vg_local[:, at] + mul(head(k, h), grad_state, NN)).astype(BF16)
        total = None
        for quad in range(MEMBERS // 4):
            piece = got[quad * 4 + (h % 2) * 2 + h // 2, :ROWS, :].astype(F32)
            total = piece if total is None else total + piece
        wg[:, at] = total


def exchange(value, axes):
    return lax.all_to_all(value, axes, 0, 0, tiled=True)


def body(queries, keys, values, out_weight, cotangent):
    group = lax.axis_index(XY).astype(jnp.int32)
    member = lax.axis_index(ZC)
    core = lax.axis_index("c")
    odd = lax.rem(lax.axis_index("z"), 2)
    me = (core * 2 + odd).astype(jnp.int32).reshape(1)
    group_id = group.reshape(1)

    base = (group * MEMBERS * TOKENS).reshape(1)
    place = member.astype(jnp.int32).reshape(1)

    def to_core(x):
        return lax.ppermute(x, "c", [(0, 1), (1, 0)])

    def to_odd(x):
        return lax.ppermute(x, "z", [(i, i ^ 1) for i in range(8)])

    def to_both(x):
        return lax.ppermute(x, ZC, [(i, i ^ 3) for i in range(MEMBERS)])

    head_block = shape((TOKENS, HEAD), BF16)
    small = 2 * TOKENS * HEAD * FEATURES
    large = 2 * TOKENS * MODEL * FEATURES
    triple = shape((3 * TOKENS, HEAD), BF16)

    sent, x0, x1, x2, x3 = call(
        keys_kernel,
        [SMEM] + [VMEM] * 4,
        [shape((MEMBERS, STATE_ROWS + ROWS, HEAD), BF16)] + [triple] * 4,
        (me, keys, values, out_weight, queries),
        small,
    )
    first = exchange(sent, ZC)
    cot_c = to_core(cotangent)
    x1, x2, x3 = to_core(x1), to_odd(x2), to_both(x3)
    inside, sent = call(
        before_kernel,
        [VMEM],
        [
            shape((MEMBERS, STATE_ROWS, HEAD), F32),
            shape((GROUPS, STATE_ROWS + SHARE, HEAD), BF16),
        ],
        (first,),
        small,
        limit=ROOM,
    )
    sent, cot_c, x1, x2, x3, late = lax.optimization_barrier((sent, cot_c, x1, x2, x3, cotangent))
    cot_z = to_odd(late)
    second = exchange(sent, XY)
    cot_zc = to_core(cot_z)
    states = call(
        carry_kernel,
        [SMEM, VMEM, VMEM],
        [shape((MEMBERS, STATE_ROWS, HEAD), BF16)],
        (group_id, second, inside),
        small,
        limit=ROOM,
    )
    third = exchange(states, ZC)
    g0, g1, g2, g3, sent = call(
        gradient_kernel,
        [SMEM] * 2 + [HBM] * 5 + [VMEM] * 4,
        [head_block] * 4
        + [shape((MEMBERS, STATE_ROWS, HEAD), BF16)],
        (base, place, cotangent, cot_c, cot_z, cot_zc, second, x0, x1, x2, x3),
        large,
        scratch_shapes=[
            pltpu.VMEM((4, TOKENS, MODEL), BF16),
            pltpu.VMEM((GROUPS, STATE_ROWS + SHARE, HEAD), BF16),
            pltpu.SemaphoreType.DMA((5,)),
        ],
    )
    third, sent, g0 = lax.optimization_barrier((third, sent, g0))
    a0, a1, a2, a3, s0, p1, p2, p3 = call(
        attend_kernel,
        [SMEM] * 2 + [VMEM] * 8,
        [head_block] * 5 + [triple] * 3,
        (base, place, x0, x1, x2, x3, third, g1, g2, g3),
        3 * small,
    )
    fourth = exchange(sent, ZC)
    width = SHARE + STATE_ROWS
    terms = pl.pallas_call(
        weight_kernel,
        in_specs=[HBM] * 4 + [VMEM] * 4,
        out_specs=HBM,
        out_shape=shape((GROUPS, width, HEAD), BF16),
        scratch_shapes=[
            pltpu.VMEM((4, TOKENS, MODEL), BF16),
            pltpu.VMEM((GROUPS, width, HEAD), BF16),
            pltpu.SemaphoreType.DMA((CHUNKS, 4)),
            pltpu.SemaphoreType.DMA((CHUNKS,)),
        ],
        compiler_params=pltpu.CompilerParams(vmem_limit_bytes=SOME),
        cost_estimate=pl.CostEstimate(flops=large, bytes_accessed=6 << 20, transcendentals=0),
    )(cotangent, cot_c, cot_z, cot_zc, a0, a1, a2, a3)
    fourth, terms = lax.optimization_barrier((fourth, terms))
    inside, total = call(
        after_kernel,
        [VMEM],
        [shape((MEMBERS, STATE_ROWS, HEAD), F32), shape((STATE_ROWS, HEAD), BF16)],
        (fourth,),
        small,
        limit=ROOM,
    )
    terms = terms.at[:, SHARE:, :].set(total[None])
    got = exchange(terms, XY)

    p1, p2, p3, weight, _ = lax.optimization_barrier((p1, p2, p3, second, total))
    w0 = [weight[: GROUPS // 2, STATE_ROWS:], weight[GROUPS // 2 :, STATE_ROWS:]]
    p1, p2, p3 = to_core(p1), to_odd(p2), to_both(p3)
    w1 = [to_core(w) for w in w0]
    ring = [(i, (i + 1) % 8) for i in range(8)]
    w2 = [lax.ppermute(w0[0], "z", ring), lax.ppermute(w0[1], "z", [(j, i) for i, j in ring])]
    got, w1 = lax.optimization_barrier((got, w1))
    back = call(
        reduce_kernel,
        [SMEM, VMEM, VMEM],
        [shape((MEMBERS, ROWS + STATE_ROWS, HEAD), BF16)],
        (group_id, got, inside),
        small,
        limit=ROOM,
    )
    back, w2, p1, p2, p3 = lax.optimization_barrier((back, w2, p1, p2, p3))
    w3 = [to_core(w) for w in w2]
    last = exchange(back, ZC)
    mixed = call(
        mixed_kernel,
        [VMEM] * 12,
        [shape((TOKENS, MODEL), BF16)],
        (a0, p1, p2, p3, *w0, *w1, *w2, *w3),
        large,
    )
    query_gradient, kg_local, vg_local = call(
        local_kernel,
        [SMEM] + [VMEM] * 8,
        [shape((TOKENS, FEATURES), BF16)] + [shape((TOKENS, FEATURES), F32)] * 2,
        (me, queries, keys, values, g0, s0, p1, p2, p3),
        6 * small,
        scratch_shapes=[pltpu.VMEM((HEADS, 2 * TOKENS, HEAD), BF16)],
    )
    last, mixed, kg_local = lax.optimization_barrier((last, mixed, kg_local))
    key_gradient, value_gradient, weight_grad = call(
        final_kernel,
        [VMEM] * 5,
        [shape((TOKENS, FEATURES), BF16)] * 2 + [shape((ROWS, FEATURES), F32)],
        (last, keys, values, kg_local, vg_local),
        2 * small,
        limit=ROOM,
    )
    return (mixed, query_gradient, key_gradient, value_gradient, weight_grad)


def solution(mesh):
    grid = Mesh(mesh.devices.reshape(4, 4, 8, 2), ("x", "y", "z", "c"))
    spec = P(("x", "y", "z", "c"), None)
    return jax.shard_map(
        body, mesh=grid, in_specs=(spec,) * 5, out_specs=(spec,) * 5, check_vma=False
    )
```

```python
import jax
import jax.numpy as jnp
from jax import lax
from jax.experimental import pallas as pl
from jax.experimental.pallas import tpu as pltpu
from jax.sharding import Mesh, PartitionSpec as P

HEADS = 4
HEAD = 128
TOKENS = 128
FEATURES = HEADS * HEAD
MODEL = 4096
GROUPS = 16
MEMBERS = 16
ROWS = MODEL // (GROUPS * MEMBERS)
SHARE = MODEL // GROUPS
STATE_ROWS = FEATURES // MEMBERS
CHUNKS = 4
PIECES = 2
LIMIT = 63_000_000
SOME = 60_000_000
ROOM = 32_000_000
SLICE = HEAD // MEMBERS
FLIPS = (0, 2, 1, 3)
XY = ("x", "y")
ZC = ("z", "c")
BF16 = jnp.bfloat16
F32 = jnp.float32
NN = (((1,), (0,)), ((), ()))
NT = (((1,), (1,)), ((), ()))
TN = (((0,), (0,)), ((), ()))
VMEM = pl.BlockSpec(memory_space=pltpu.VMEM)
SMEM = pl.BlockSpec(memory_space=pltpu.SMEM)
HBM = pl.BlockSpec(memory_space=pl.ANY)


def mul(a, b, dims):
    return lax.dot_general(a, b, dims, preferred_element_type=F32)


def shape(dims, dtype):
    return jax.ShapeDtypeStruct(dims, dtype)


def call(kernel, ins, outs, args, flops, limit=LIMIT, **kw):
    out_bytes = sum(o.size * o.dtype.itemsize for o in outs)
    in_bytes = sum(a.size * a.dtype.itemsize for a in args)
    one = len(outs) == 1
    return pl.pallas_call(
        kernel,
        in_specs=ins,
        out_specs=VMEM if one else [VMEM] * len(outs),
        out_shape=outs[0] if one else outs,
        compiler_params=pltpu.CompilerParams(vmem_limit_bytes=limit),
        cost_estimate=pl.CostEstimate(
            flops=flops, bytes_accessed=in_bytes + out_bytes, transcendentals=0
        ),
        **kw,
    )(*args)


def head(ref, h):
    return ref[:, h * HEAD : (h + 1) * HEAD]


def scale_from(first):
    token = first + lax.broadcasted_iota(jnp.int32, (TOKENS, HEAD), 0)
    return lax.rsqrt((HEAD * (token + 1)).astype(F32))


def causal(x):
    row = lax.broadcasted_iota(jnp.int32, x.shape, 0)
    col = lax.broadcasted_iota(jnp.int32, x.shape, 1)
    return jnp.where(row >= col, x, 0.0).astype(BF16)


def keys_kernel(me, k, v, w, q, out, x0, x1, x2, x3):
    products = [mul(head(k, h), head(v, h), TN) for h in range(HEADS)]
    for m in range(MEMBERS):
        rows = [x[m * SLICE : (m + 1) * SLICE] for x in products]
        out[m, :STATE_ROWS, :] = jnp.concatenate(rows, axis=0).astype(BF16)
        out[m, STATE_ROWS:, :] = head(w, head_of(m))
    for flip, ref in zip(FLIPS, (x0, x1, x2, x3)):
        at = head_at(me[0] ^ flip)
        for i, x in enumerate((q, k, v)):
            ref[i * TOKENS : (i + 1) * TOKENS, :] = x[:, at]


def head_of(m):
    return (m % 2) * 2 + (m % 4) // 2


def head_at(h):
    return pl.ds(pl.multiple_of(h * HEAD, HEAD), HEAD)


def before_kernel(first, inside, send):
    running = jnp.zeros((STATE_ROWS, HEAD), F32)
    rows = []
    for m in range(MEMBERS):
        inside[m] = running
        running = running + first[m, :STATE_ROWS, :].astype(F32)
        rows.append(first[m, STATE_ROWS:, :])
    packed = jnp.concatenate([running.astype(BF16)] + rows, axis=0)
    for j in range(GROUPS):
        send[j] = packed


def carry_kernel(group, second, inside, out):
    carried = jnp.zeros((STATE_ROWS, HEAD), F32)
    for j in range(GROUPS):
        piece = second[j, :STATE_ROWS, :].astype(F32)
        carried = carried + jnp.where(j < group[0], piece, 0.0)
    states = [inside[m] + carried for m in range(MEMBERS)]
    for m in range(MEMBERS):
        at = head_of(m) * SLICE
        rows = [states[m ^ k][at : at + SLICE] for k in range(4)]
        out[m] = jnp.concatenate(rows, axis=0).astype(BF16)


def attend_kernel(
    base, place, x0, x1, x2, x3, got, g1, g2, g3, a0, a1, a2, a3, s0, p1, p2, p3
):
    slices = [got[m].astype(F32) for m in range(MEMBERS)]
    for i, (x, a) in enumerate(zip((x0, x1, x2, x3), (a0, a1, a2, a3))):
        rows = [piece[i * SLICE : (i + 1) * SLICE] for piece in slices]
        key_state = jnp.concatenate(rows, axis=0).astype(BF16)
        q, k, v = (x[j * TOKENS : (j + 1) * TOKENS, :] for j in range(3))
        scores = causal(mul(q, k, NT))
        total = mul(scores, v, NN) + mul(q, key_state, NN)
        result = (total * scale_from(base[0] + (place[0] ^ i) * TOKENS)).astype(BF16)
        a[...] = result
        if i == 0:
            s0[...] = key_state
        else:
            pair, g = ((p1, g1), (p2, g2), (p3, g3))[i - 1]
            pair[:TOKENS] = result
            pair[TOKENS : 2 * TOKENS] = g[...]
            pair[2 * TOKENS :] = key_state


def gradient_kernel(
    base, place, c0, c1, c2, c3, w, x0, x1, x2, x3, g0, g1, g2, g3, out, cots, held, sems
):
    copies = [
        pltpu.make_async_copy(c, cots.at[i], sems.at[i]) for i, c in enumerate((c0, c1, c2, c3))
    ]
    weight_copy = pltpu.make_async_copy(w, held, sems.at[4])
    weight_copy.start()
    for copy in copies:
        copy.start()
    weight_copy.wait()
    right = held[:, STATE_ROWS:, :].reshape(MODEL, HEAD)
    sums = []
    for i, (x, g) in enumerate(zip((x0, x1, x2, x3), (g0, g1, g2, g3))):
        copies[i].wait()
        scale = scale_from(base[0] + (place[0] ^ i) * TOKENS)
        total = mul(cots[i], right, NN)
        value = (total * scale).astype(BF16)
        g[...] = value
        sums.append(mul(x[:TOKENS, :], value, TN))
    for m in range(MEMBERS):
        at = slice(m * SLICE, (m + 1) * SLICE)
        out[m] = jnp.concatenate([x[at] for x in sums], axis=0).astype(BF16)


def after_kernel(first, inside, total):
    pieces = [first[m].astype(F32) for m in range(MEMBERS)]
    running = jnp.zeros((STATE_ROWS, HEAD), F32)
    for block in reversed(range(MEMBERS)):
        quad, local = block // 4, block % 4
        inside[block] = running
        rows = []
        for h in range(HEADS):
            place = (h % 2) * 2 + h // 2
            at = (place ^ local) * SLICE
            rows.append(pieces[quad * 4 + place][at : at + SLICE])
        running = running + jnp.concatenate(rows, axis=0)
    total[...] = running.astype(BF16)


def mixed_kernel(a0, p1, p2, p3, *refs):
    *parts, out = refs
    left = jnp.concatenate([a0[...]] + [p[:TOKENS] for p in (p1, p2, p3)], axis=1)
    for j in range(GROUPS):
        half, at = divmod(j, GROUPS // 2)
        right = jnp.concatenate([w[at] for w in parts[half::2]], axis=1)
        out[:, j * SHARE : (j + 1) * SHARE] = mul(left, right, NT).astype(BF16)


def weight_kernel(c0, c1, c2, c3, a0, a1, a2, a3, out, cots, result, sems, out_sems):
    width = MODEL // PIECES
    part = GROUPS // PIECES
    copies = []
    for step in range(PIECES):
        at = pl.ds(step * width, width)
        copies.append(
            [
                pltpu.make_async_copy(c.at[:, at], cots.at[i, :, at], sems.at[step, i])
                for i, c in enumerate((c0, c1, c2, c3))
            ]
        )
    for group in copies:
        for copy in group:
            copy.start()
    turned = jnp.concatenate([a[...].T for a in (a0, a1, a2, a3)], axis=1)
    backs = []
    for step in range(PIECES):
        for copy in copies[step]:
            copy.wait()
        for j in range(step * part, (step + 1) * part):
            at = slice(j * SHARE, (j + 1) * SHARE)
            right = cots[:, :, at].reshape(4 * TOKENS, SHARE)
            term = mul(turned, right, NN).astype(BF16)
            for half in range(2):
                result[j, half * HEAD : (half + 1) * HEAD, :] = term[
                    :, half * HEAD : (half + 1) * HEAD
                ]
            result[j, SHARE:, :] = jnp.zeros((STATE_ROWS, HEAD), BF16)
        at = pl.ds(step * part, part)
        backs.append(pltpu.make_async_copy(result.at[at], out.at[at], out_sems.at[step]))
        backs[-1].start()
    for back in backs:
        back.wait()


def local_kernel(me, q, k, v, g0, s0, p1, p2, p3, qg, kg, vg, by_head):
    by_head[me[0], :TOKENS] = g0[...]
    by_head[me[0], TOKENS:] = s0[...]
    for flip, pair in zip(FLIPS[1:], (p1, p2, p3)):
        by_head[me[0] ^ flip] = pair[TOKENS:]
    for h in range(HEADS):
        at = slice(h * HEAD, (h + 1) * HEAD)
        qh, kh, vh, gh = head(q, h), head(k, h), head(v, h), by_head[h, :TOKENS]
        scores = causal(mul(qh, kh, NT))
        grads = causal(mul(gh, vh, NT))
        qg[:, at] = (mul(grads, kh, NN) + mul(gh, by_head[h, TOKENS:], NT)).astype(BF16)
        kg[:, at] = mul(grads, qh, TN)
        vg[:, at] = mul(scores, gh, TN)


def reduce_kernel(group, got, inside, out):
    after = jnp.zeros((STATE_ROWS, HEAD), F32)
    for j in range(GROUPS):
        piece = got[j, SHARE:, :].astype(F32)
        after = after + jnp.where(j > group[0], piece, 0.0)
    for m in range(MEMBERS):
        out[m, ROWS:, :] = (inside[m] + after).astype(BF16)
    per = HEAD // ROWS
    for half in range(2):
        total = None
        for j in range(GROUPS):
            piece = got[j, half * HEAD : (half + 1) * HEAD, :].astype(F32)
            total = piece if total is None else total + piece
        turned = total.T.astype(BF16)
        for m in range(per):
            out[half * per + m, :ROWS, :] = turned[m * ROWS : (m + 1) * ROWS]


def final_kernel(got, k, v, kg_local, vg_local, kg, vg, wg):
    states = [got[m, ROWS:, :].astype(F32) for m in range(MEMBERS)]
    for h in range(HEADS):
        at = slice(h * HEAD, (h + 1) * HEAD)
        rows = [x[h * SLICE : (h + 1) * SLICE] for x in states]
        grad_state = jnp.concatenate(rows, axis=0).astype(BF16)
        kg[:, at] = (kg_local[:, at] + mul(head(v, h), grad_state, NT)).astype(BF16)
        vg[:, at] = (vg_local[:, at] + mul(head(k, h), grad_state, NN)).astype(BF16)
        total = None
        for quad in range(MEMBERS // 4):
            piece = got[quad * 4 + (h % 2) * 2 + h // 2, :ROWS, :].astype(F32)
            total = piece if total is None else total + piece
        wg[:, at] = total


def exchange(value, axes):
    return lax.all_to_all(value, axes, 0, 0, tiled=True)


def body(queries, keys, values, out_weight, cotangent):
    group = lax.axis_index(XY).astype(jnp.int32)
    member = lax.axis_index(ZC)
    core = lax.axis_index("c")
    odd = lax.rem(lax.axis_index("z"), 2)
    me = (core * 2 + odd).astype(jnp.int32).reshape(1)
    group_id = group.reshape(1)

    base = (group * MEMBERS * TOKENS).reshape(1)
    place = member.astype(jnp.int32).reshape(1)

    def to_core(x):
        return lax.ppermute(x, "c", [(0, 1), (1, 0)])

    def to_odd(x):
        return lax.ppermute(x, "z", [(i, i ^ 1) for i in range(8)])

    def to_both(x):
        return lax.ppermute(x, ZC, [(i, i ^ 3) for i in range(MEMBERS)])

    head_block = shape((TOKENS, HEAD), BF16)
    small = 2 * TOKENS * HEAD * FEATURES
    large = 2 * TOKENS * MODEL * FEATURES
    triple = shape((3 * TOKENS, HEAD), BF16)

    sent, x0, x1, x2, x3 = call(
        keys_kernel,
        [SMEM] + [VMEM] * 4,
        [shape((MEMBERS, STATE_ROWS + ROWS, HEAD), BF16)] + [triple] * 4,
        (me, keys, values, out_weight, queries),
        small,
    )
    first = exchange(sent, ZC)
    cot_c = to_core(cotangent)
    x1, x2, x3 = to_core(x1), to_odd(x2), to_both(x3)
    inside, sent = call(
        before_kernel,
        [VMEM],
        [
            shape((MEMBERS, STATE_ROWS, HEAD), F32),
            shape((GROUPS, STATE_ROWS + SHARE, HEAD), BF16),
        ],
        (first,),
        small,
        limit=ROOM,
    )
    sent, cot_c, x1, x2, x3, late = lax.optimization_barrier((sent, cot_c, x1, x2, x3, cotangent))
    cot_z = to_odd(late)
    second = exchange(sent, XY)
    cot_zc = to_core(cot_z)
    states = call(
        carry_kernel,
        [SMEM, VMEM, VMEM],
        [shape((MEMBERS, STATE_ROWS, HEAD), BF16)],
        (group_id, second, inside),
        small,
        limit=ROOM,
    )
    third = exchange(states, ZC)
    g0, g1, g2, g3, sent = call(
        gradient_kernel,
        [SMEM] * 2 + [HBM] * 5 + [VMEM] * 4,
        [head_block] * 4
        + [shape((MEMBERS, STATE_ROWS, HEAD), BF16)],
        (base, place, cotangent, cot_c, cot_z, cot_zc, second, x0, x1, x2, x3),
        large,
        scratch_shapes=[
            pltpu.VMEM((4, TOKENS, MODEL), BF16),
            pltpu.VMEM((GROUPS, STATE_ROWS + SHARE, HEAD), BF16),
            pltpu.SemaphoreType.DMA((5,)),
        ],
    )
    third, sent, g0 = lax.optimization_barrier((third, sent, g0))
    a0, a1, a2, a3, s0, p1, p2, p3 = call(
        attend_kernel,
        [SMEM] * 2 + [VMEM] * 8,
        [head_block] * 5 + [triple] * 3,
        (base, place, x0, x1, x2, x3, third, g1, g2, g3),
        3 * small,
    )
    fourth = exchange(sent, ZC)
    width = SHARE + STATE_ROWS
    terms = pl.pallas_call(
        weight_kernel,
        in_specs=[HBM] * 4 + [VMEM] * 4,
        out_specs=HBM,
        out_shape=shape((GROUPS, width, HEAD), BF16),
        scratch_shapes=[
            pltpu.VMEM((4, TOKENS, MODEL), BF16),
            pltpu.VMEM((GROUPS, width, HEAD), BF16),
            pltpu.SemaphoreType.DMA((PIECES, 4)),
            pltpu.SemaphoreType.DMA((PIECES,)),
        ],
        compiler_params=pltpu.CompilerParams(vmem_limit_bytes=SOME),
        cost_estimate=pl.CostEstimate(flops=large, bytes_accessed=6 << 20, transcendentals=0),
    )(cotangent, cot_c, cot_z, cot_zc, a0, a1, a2, a3)
    fourth, terms = lax.optimization_barrier((fourth, terms))
    inside, total = call(
        after_kernel,
        [VMEM],
        [shape((MEMBERS, STATE_ROWS, HEAD), F32), shape((STATE_ROWS, HEAD), BF16)],
        (fourth,),
        small,
        limit=ROOM,
    )
    terms = terms.at[:, SHARE:, :].set(total[None])
    got = exchange(terms, XY)

    p1, p2, p3, weight, _ = lax.optimization_barrier((p1, p2, p3, second, total))
    w0 = [weight[: GROUPS // 2, STATE_ROWS:], weight[GROUPS // 2 :, STATE_ROWS:]]
    p1, p2, p3 = to_core(p1), to_odd(p2), to_both(p3)
    w0, p1 = lax.optimization_barrier((w0, p1))
    w1 = [to_core(w) for w in w0]
    ring = [(i, (i + 1) % 8) for i in range(8)]
    w2 = [lax.ppermute(w0[0], "z", ring), lax.ppermute(w0[1], "z", [(j, i) for i, j in ring])]
    got, w1 = lax.optimization_barrier((got, w1))
    back = call(
        reduce_kernel,
        [SMEM, VMEM, VMEM],
        [shape((MEMBERS, ROWS + STATE_ROWS, HEAD), BF16)],
        (group_id, got, inside),
        small,
        limit=ROOM,
    )
    back, w2, p1, p2, p3 = lax.optimization_barrier((back, w2, p1, p2, p3))
    w3 = [to_core(w) for w in w2]
    last = exchange(back, ZC)
    mixed = call(
        mixed_kernel,
        [VMEM] * 12,
        [shape((TOKENS, MODEL), BF16)],
        (a0, p1, p2, p3, *w0, *w1, *w2, *w3),
        large,
    )
    query_gradient, kg_local, vg_local = call(
        local_kernel,
        [SMEM] + [VMEM] * 8,
        [shape((TOKENS, FEATURES), BF16)] + [shape((TOKENS, FEATURES), F32)] * 2,
        (me, queries, keys, values, g0, s0, p1, p2, p3),
        6 * small,
        scratch_shapes=[pltpu.VMEM((HEADS, 2 * TOKENS, HEAD), BF16)],
    )
    last, mixed, kg_local = lax.optimization_barrier((last, mixed, kg_local))
    key_gradient, value_gradient, weight_grad = call(
        final_kernel,
        [VMEM] * 5,
        [shape((TOKENS, FEATURES), BF16)] * 2 + [shape((ROWS, FEATURES), F32)],
        (last, keys, values, kg_local, vg_local),
        2 * small,
        limit=ROOM,
    )
    return (mixed, query_gradient, key_gradient, value_gradient, weight_grad)


def solution(mesh):
    grid = Mesh(mesh.devices.reshape(4, 4, 8, 2), ("x", "y", "z", "c"))
    spec = P(("x", "y", "z", "c"), None)
    return jax.shard_map(
        body, mesh=grid, in_specs=(spec,) * 5, out_specs=(spec,) * 5, check_vma=False
    )
```
